256 devices in a mesh: ctx: 32 (over z, y), kvh: 8 (over x, core).
Axes of the slice: x: 4, y: 4, z: 8, core: 2. Of those that a mesh axis runs over, the one named last changes fastest.
Arguments:
- queries: bfloat16 [128, 8, 8, 128], P('ctx', 'kvh')
- new_keys: bfloat16 [128, 8, 128], P('ctx', 'kvh')
- new_values: bfloat16 [128, 8, 128], P('ctx', 'kvh'), may hold values from -6 to 6
- cache_keys: bfloat16 [8, 131072, 128], P('kvh', 'ctx')
- cache_values: bfloat16 [8, 131072, 128], P('kvh', 'ctx')
- cache_lengths: int32 [32], P('ctx'), may hold values from 1024 to 4096, as said below
- offsets: int32 [128], replicated, may hold values from 0 to 127, each once
Outputs:
- attended: float32 [128, 8192], P('ctx')
The draws below stay inside these ranges and needn't reach their ends.
Inputs may be any that keep to these rules, and one draw needn't show every extreme that they name: `cache_lengths`: at least 1024 filled positions in every shard; some shard is full in every draw. `offsets`: each value once.
All inputs are finite; a program needn't handle non-finite values.
Results may differ from the reference program's by a relative error of at most 0.00065.
Values may be sent and summed in bfloat16 or wider, within the bound.
No kernel may reach another device: no remote copies, remote signals or barrier semaphores. Data moves between devices by JAX's collectives and lax.ppermute only.
A program may use at most 64 MiB of HBM per device.

```python
import jax
import jax.numpy as jnp
from jax import lax

KVH = 8
G = 8
HD = 128
NEW = 128
CACHE_DEV = 4096
KBLK = 512
CACHE = 131072
N_CTX = 32


def shared_rows(key):
    own_part = jax.random.normal(key, (NEW, KVH, HD), jnp.float32)
    base = own_part
    return base


def draw_queries(key, part):
    base = shared_rows(key)
    key = jax.random.fold_in(key, 1)
    noise = jax.random.normal(key, (NEW, KVH, G, HD), jnp.float32)
    return (base[:, :, None, :] + 0.3 * noise).astype(jnp.bfloat16)


def draw_new_keys(key, part):
    base = shared_rows(key)
    key = jax.random.fold_in(key, 2)
    noise = jax.random.normal(key, (NEW, KVH, HD), jnp.float32)
    return (base + 0.3 * noise).astype(jnp.bfloat16)


def draw_cache_keys(key, part):
    key = jax.random.fold_in(key, 6)
    keys = jax.random.normal(key, (KVH, CACHE, HD), jnp.float32)
    return keys.astype(jnp.bfloat16)


def draw_cache_values(key, part):
    key = jax.random.fold_in(key, 3)
    width = CACHE_DEV // 8
    noise = jax.random.normal(key, (KVH, CACHE // width, width, HD), jnp.float32)
    shifts = jax.random.uniform(jax.random.fold_in(key, 5), (KVH, CACHE // width, 1, HD), jnp.float32, -3.0, 3.0)
    return (noise + shifts).reshape(KVH, CACHE, HD).astype(jnp.bfloat16)


def draw_cache_lengths(key, part):
    key = jax.random.fold_in(key, 4)
    filled = jax.random.randint(key, (N_CTX,), CACHE_DEV // 4, CACHE_DEV + 1, jnp.int32)
    picked = jax.random.randint(jax.random.fold_in(key, 7), (), 0, N_CTX, jnp.int32)
    return jnp.where(jnp.arange(N_CTX, dtype=jnp.int32) == picked, CACHE_DEV, filled).astype(jnp.int32)


def level_of(stream_key, shape, cuts, least, largest):
    factor_of = 1.0
    for dim, parts in cuts:
        heights = jax.random.uniform(jax.random.fold_in(jax.random.fold_in(stream_key, 6), dim), (parts,), jnp.float32, least / len(cuts), largest / len(cuts))
        factor_of = factor_of * jnp.repeat(jnp.exp(heights), shape[dim] // parts).reshape((-1,) + (1,) * (len(shape) - 1 - dim))
    return factor_of


def bell_draw(own_key, shape, scale, limit, split=(), kind=jnp.bfloat16):
    values = scale * jax.random.normal(own_key, shape, jnp.float32)
    if split:
        values = values * level_of(own_key, shape, split, -0.22, 0.18)
    return jnp.clip(values, -limit, limit).astype(kind)


def setup_inputs(seed: int = 0) -> dict:
    key_of = jax.random.split(jax.random.key(seed), 8)
    queries = draw_queries(jax.random.fold_in(key_of[7], 71), 0)
    new_keys = draw_new_keys(jax.random.fold_in(key_of[7], 71), 0)
    new_values = bell_draw(key_of[2], (NEW, KVH, HD), 1.0, 6.0, ((0, 32), (1, 8)))
    cache_keys = draw_cache_keys(jax.random.fold_in(key_of[7], 71), 0)
    cache_values = draw_cache_values(jax.random.fold_in(key_of[7], 71), 0)
    cache_lengths = draw_cache_lengths(jax.random.fold_in(key_of[7], 71), 0)
    offsets = jax.random.permutation(key_of[6], NEW).astype(jnp.int32)
    return {"queries": queries, "new_keys": new_keys, "new_values": new_values, "cache_keys": cache_keys, "cache_values": cache_values, "cache_lengths": cache_lengths, "offsets": offsets}


NEG = -1e30


def block_stats(query, keys, values, valid):
    scale = query.shape[-1] ** -0.5
    scores = jnp.einsum("nhgd,khd->nhgk", query.astype(jnp.float32), keys.astype(jnp.float32)) * scale
    scores = jnp.where(valid, scores, NEG)
    top = jnp.max(scores, axis=-1)
    probs = jnp.where(valid, jnp.exp(scores - top[..., None]), 0.0).astype(jnp.bfloat16)
    total = jnp.sum(probs.astype(jnp.float32), axis=-1)
    output = jnp.einsum("nhgk,khd->nhgd", probs.astype(jnp.float32), values.astype(jnp.float32))
    return output, top, total


def combine(first, second):
    out_a, top_a, tot_a = first
    out_b, top_b, tot_b = second
    upper = jnp.maximum(top_a, top_b)
    wa = jnp.exp(top_a - upper)
    wb = jnp.exp(top_b - upper)
    return out_a * wa[..., None] + out_b * wb[..., None], upper, tot_a * wa + tot_b * wb


def reference(queries, new_keys, new_values, cache_keys, cache_values, cache_lengths, offsets):
    blocks = CACHE // KBLK
    keys_t = jnp.transpose(cache_keys, (1, 0, 2))
    values_t = jnp.transpose(cache_values, (1, 0, 2))
    init = (jnp.zeros(queries.shape, jnp.float32), jnp.full(queries.shape[:3], NEG, jnp.float32), jnp.zeros(queries.shape[:3], jnp.float32))

    def step(index, carry):
        start = (index * KBLK).astype(jnp.int32)
        kblock = lax.dynamic_slice_in_dim(keys_t, start, KBLK, 0)
        vblock = lax.dynamic_slice_in_dim(values_t, start, KBLK, 0)
        position = start + jnp.arange(KBLK, dtype=jnp.int32)
        shard = position // CACHE_DEV
        valid = (position % CACHE_DEV) < jnp.take(cache_lengths, shard)
        return combine(carry, block_stats(queries, kblock, vblock, valid[None, None, None, :]))

    state = lax.fori_loop(0, blocks, step, init)
    visible = offsets[None, :] <= offsets[:, None]
    state = combine(state, block_stats(queries, new_keys, new_values, visible[:, None, None, :]))
    result = state[0] / state[2][..., None]
    return result.reshape(NEW, KVH * G * HD)
```

```python
import math

import jax
import jax.numpy as jnp
from jax import lax
from jax.experimental import pallas as pl
from jax.experimental.pallas import tpu as pltpu
from jax.sharding import PartitionSpec as P

KBLK = 512
NEG = -1e30
LANES = 128
STAT_ROWS = 8
NT = (((1,), (1,)), ((), ()))
VMEM_LIMIT = 56 * 2**20


def attend_kernel(length_ref, q_ref, k_ref, v_ref, nk_ref, nv_ref, vis_ref, out_ref, ks_ref, vs_ref):
    positions, width = k_ref.shape
    rows = q_ref.shape[0]
    chunks, chunk_rows, _ = out_ref.shape
    per = rows // chunks
    groups = per // 8
    factor = width**-0.5 * math.log2(math.e)
    length = length_ref[0]
    blocks = positions // KBLK

    def fill(b, carry):
        at = pl.multiple_of(b * KBLK, KBLK)
        here = pl.ds(at, KBLK)

        @pl.when(at + KBLK <= length)
        def _():
            ks_ref[here, :] = k_ref[here, :]
            vs_ref[here, :width] = v_ref[here, :]
            vs_ref[here, width:] = jnp.ones((KBLK, width), vs_ref.dtype)

        @pl.when(at + KBLK > length)
        def _():
            inside = at + lax.broadcasted_iota(jnp.int32, (KBLK, width), 0) < length
            first = k_ref[0:16, :].astype(jnp.float32)[0:1, :]
            keys = jnp.where(inside, k_ref[here, :].astype(jnp.float32), first)
            values = jnp.where(inside, v_ref[here, :].astype(jnp.float32), 0.0)
            ks_ref[here, :] = keys.astype(ks_ref.dtype)
            vs_ref[here, :width] = values.astype(vs_ref.dtype)
            vs_ref[here, width:] = jnp.where(inside, 1.0, 0.0).astype(vs_ref.dtype)

        return carry

    lax.fori_loop(0, blocks, fill, 0)

    query = q_ref[...]
    top = jnp.full((rows, 1), NEG, jnp.float32)
    acc = jnp.zeros((rows, 2 * width), jnp.float32)
    for b in range(blocks):
        here = slice(b * KBLK, (b + 1) * KBLK)
        scores = lax.dot_general(query, ks_ref[here, :], NT, preferred_element_type=jnp.float32)
        block_top = jnp.max(scores, axis=1, keepdims=True)
        probs = jnp.exp2(scores * factor - block_top * factor).astype(jnp.bfloat16)
        part = jnp.dot(probs, vs_ref[here, :], preferred_element_type=jnp.float32)
        upper = jnp.maximum(top, block_top)
        acc = acc * jnp.exp2((top - upper) * factor) + part * jnp.exp2((block_top - upper) * factor)
        top = upper

    scores = lax.dot_general(query, nk_ref[...], NT, preferred_element_type=jnp.float32)
    seen = jnp.broadcast_to(vis_ref[...][:, None, :], (rows // 8, 8, LANES)).reshape(rows, LANES) > 0
    scores = jnp.where(seen, scores, NEG)
    upper = jnp.maximum(top, jnp.max(scores, axis=1, keepdims=True))
    probs = jnp.where(seen, jnp.exp2((scores - upper) * factor), 0.0)
    rounded = probs.astype(jnp.bfloat16)
    lane = lax.broadcasted_iota(jnp.int32, (rows, LANES), 1)
    both = jnp.where(lane < 4, rounded.astype(jnp.float32), probs - rounded.astype(jnp.float32))
    part = jnp.dot(both.astype(jnp.bfloat16), nv_ref[...], preferred_element_type=jnp.float32)
    acc = acc * jnp.exp2((top - upper) * factor) + part
    top = jnp.broadcast_to(upper, (rows, LANES))

    lane8 = lax.broadcasted_iota(jnp.int32, (8, LANES), 1)
    for c in range(chunks):
        out_ref[c, :per, :] = acc[c * per : (c + 1) * per, :width]
        stat = jnp.zeros((8, LANES), jnp.float32)
        for v in range(groups):
            at = slice(c * per + v * 8, c * per + v * 8 + 8)
            stat = jnp.where(lane8 == v, top[at, :], stat)
            stat = jnp.where(lane8 == groups + v, acc[at, width:], stat)
        out_ref[c, per:, :] = stat


def merge_kernel(in_ref, out_ref, row_ref):
    sources, chunk_rows, width = in_ref.shape
    copies, rows, _ = out_ref.shape
    per = chunk_rows - STAT_ROWS
    groups = per // 8
    factor = width**-0.5 * math.log2(math.e)
    stat = in_ref[:, per:, :]
    for v in range(groups):
        tops = jnp.broadcast_to(stat[:, :, v : v + 1], (sources, 8, width))
        totals = jnp.broadcast_to(stat[:, :, groups + v : groups + v + 1], (sources, 8, width))
        upper = jnp.max(tops, axis=0)
        weight = jnp.exp2((tops - upper[None]) * factor)
        out = jnp.sum(in_ref[:, v * 8 : v * 8 + 8, :] * weight, axis=0)
        out = out / jnp.sum(totals * weight, axis=0)
        for g in range(8):
            row_ref[v : v + 1, g * width : (g + 1) * width] = out[g : g + 1, :]
    row = row_ref[...]
    for c in range(copies):
        out_ref[c] = row


def shards(queries, new_keys, new_values, cache_keys, cache_values, cache_lengths, offsets):
    count = lax.axis_size("ctx")
    heads = lax.axis_size("kvh")
    myself = lax.axis_index("ctx")
    rows, _, group, width = queries.shape
    total = count * rows * group
    per = rows * group
    vmem = pl.BlockSpec(memory_space=pltpu.VMEM)
    smem = pl.BlockSpec(memory_space=pltpu.SMEM)
    params = pltpu.CompilerParams(vmem_limit_bytes=VMEM_LIMIT)

    with jax.named_scope("gather_queries"):
        mine = queries.reshape(per, width)
        every = lax.all_to_all(jnp.broadcast_to(mine[None], (count, per, width)), "ctx", 0, 0)
        every = every.reshape(total, width)

    with jax.named_scope("own_new_tokens"):
        key_rows = new_keys[:, 0, :]
        value_rows = jnp.concatenate([new_values[:, 0, :], jnp.ones((rows, width), new_values.dtype)], axis=1)
        pad = LANES - 2 * rows
        key_rows = jnp.pad(jnp.concatenate([key_rows, key_rows]), ((0, pad), (0, 0)))
        value_rows = jnp.pad(jnp.concatenate([value_rows, value_rows]), ((0, pad), (0, 0)))
        own = lax.dynamic_slice_in_dim(offsets, myself * rows, rows, 0)
        own = jnp.pad(jnp.concatenate([own, own]), (0, pad), constant_values=2**30)
        visible = (own[None, :] <= offsets[:, None]).astype(jnp.float32)

    with jax.named_scope("attend"):
        partial = pl.pallas_call(
            attend_kernel,
            out_shape=jax.ShapeDtypeStruct((count, per + STAT_ROWS, width), jnp.float32),
            in_specs=[smem] + [vmem] * 6,
            out_specs=vmem,
            scratch_shapes=[
                pltpu.VMEM(cache_keys.shape[1:], cache_keys.dtype),
                pltpu.VMEM((cache_keys.shape[1], 2 * width), cache_keys.dtype),
            ],
            compiler_params=params,
        )(cache_lengths, every, cache_keys[0], cache_values[0], key_rows, value_rows, visible)

    with jax.named_scope("exchange_partials"):
        arrived = lax.all_to_all(partial, "ctx", 0, 0)

    with jax.named_scope("merge"):
        merged = pl.pallas_call(
            merge_kernel,
            out_shape=jax.ShapeDtypeStruct((heads, rows, group * width), jnp.float32),
            in_specs=[vmem],
            out_specs=vmem,
            scratch_shapes=[pltpu.VMEM((rows, group * width), jnp.float32)],
            compiler_params=params,
        )(arrived)

    with jax.named_scope("gather_heads"):
        whole = lax.all_to_all(merged, "kvh", 0, 0)
        return jnp.transpose(whole, (1, 0, 2)).reshape(rows, heads * group * width)


def solution(mesh):
    return jax.shard_map(
        shards,
        mesh=mesh,
        in_specs=(
            P("ctx", "kvh", None, None),
            P("ctx", "kvh", None),
            P("ctx", "kvh", None),
            P("kvh", "ctx", None),
            P("kvh", "ctx", None),
            P("ctx"),
            P(),
        ),
        out_specs=P("ctx", None),
        check_vma=False,
    )
```

```python
import functools
import math

import jax
import jax.numpy as jnp
from jax import lax
from jax.experimental import pallas as pl
from jax.experimental.pallas import tpu as pltpu
from jax.sharding import Mesh
from jax.sharding import PartitionSpec as P

KBLK = 512
NEG = -1e30
LANES = 128
STAT = 8
NT = (((1,), (1,)), ((), ()))
Z, Y, X, CORE = 8, 4, 4, 2
VMEM_LIMIT = 24 * 2**20


def log2_scale(width):
    return width**-0.5 * math.log2(math.e)


def prepare_kernel(place_ref, length_ref, offsets_ref, k_ref, v_ref, new_ref, ks_ref, vs_ref, vis_ref):
    positions, width = k_ref.shape
    fresh = new_ref.shape[0] // 2
    length = length_ref[0]
    ones = jnp.ones((KBLK, width), vs_ref.dtype)
    for b in range(positions // KBLK):
        here = slice(b * KBLK, (b + 1) * KBLK)

        @pl.when((b + 1) * KBLK <= length)
        def _():
            ks_ref[here, :] = k_ref[here, :]
            vs_ref[here, :width] = v_ref[here, :]
            vs_ref[here, width:] = ones

        @pl.when((b + 1) * KBLK > length)
        def _():
            inside = b * KBLK + lax.broadcasted_iota(jnp.int32, (KBLK, width), 0) < length
            first = k_ref[0:16, :].astype(jnp.float32)[0:1, :]
            keys = jnp.where(inside, k_ref[here, :].astype(jnp.float32), first)
            values = jnp.where(inside, v_ref[here, :].astype(jnp.float32), 0.0)
            ks_ref[here, :] = keys.astype(ks_ref.dtype)
            vs_ref[here, :width] = values.astype(vs_ref.dtype)
            vs_ref[here, width:] = jnp.where(inside, 1.0, 0.0).astype(vs_ref.dtype)

    row = lax.broadcasted_iota(jnp.int32, (LANES, width), 0)
    keys = jnp.zeros((LANES, width), jnp.float32)
    values = jnp.zeros((LANES, width), jnp.float32)
    new = new_ref[...].astype(jnp.float32)
    for j in range(2 * fresh):
        n = j % fresh
        keys = jnp.where(row == j, new[n : n + 1, :], keys)
        values = jnp.where(row == j, new[fresh + n : fresh + n + 1, :], values)
    ks_ref[positions:, :] = keys.astype(ks_ref.dtype)
    vs_ref[positions:, :width] = values.astype(vs_ref.dtype)
    vs_ref[positions:, width:] = jnp.where(row < 2 * fresh, 1.0, 0.0).astype(vs_ref.dtype)

    lane = lax.broadcasted_iota(jnp.int32, (1, LANES), 1)
    mine = jnp.full((1, LANES), 2**30, jnp.int32)
    start = (place_ref[0] * Y + place_ref[1]) * fresh
    for j in range(2 * fresh):
        mine = jnp.where(lane == j, offsets_ref[start + j % fresh], mine)
    for y in range(Y):
        for z in range(Z):
            for n in range(fresh):
                seen = mine <= offsets_ref[(z * Y + y) * fresh + n]
                vis_ref[y, z * fresh + n : z * fresh + n + 1, :] = jnp.where(seen, 1.0, 0.0)


def attend_kernel(backs, place_ref, q_ref, ks_ref, vs_ref, vis_ref, *refs):
    peers, _, per, width = q_ref.shape
    block = peers * per
    rows = block * len(backs)
    out_refs = refs[-len(backs) :]
    owners = [lax.rem(place_ref[1] + Y - back, Y) for back in backs]
    positions = ks_ref.shape[0] - LANES
    groups = block // 8
    factor = log2_scale(width)
    query = jnp.concatenate([q_ref[:, owner].reshape(block, width) for owner in owners], axis=0)

    scores = lax.dot_general(query, ks_ref[positions:, :], NT, preferred_element_type=jnp.float32)
    seen = jnp.concatenate([vis_ref[owner] for owner in owners], axis=0)
    seen = jnp.broadcast_to(seen[:, None, :], (rows // 8, 8, LANES)).reshape(rows, LANES) > 0
    scores = jnp.where(seen, scores, NEG)
    top = jnp.max(scores, axis=1, keepdims=True)
    probs = jnp.where(seen, jnp.exp2((scores - top) * factor), 0.0)
    rounded = probs.astype(jnp.bfloat16).astype(jnp.float32)
    lane = lax.broadcasted_iota(jnp.int32, (rows, LANES), 1)
    both = jnp.where(lane < 4, rounded, probs - rounded).astype(jnp.bfloat16)
    acc = jnp.dot(both, vs_ref[positions:, :], preferred_element_type=jnp.float32)

    for b in range(positions // KBLK):
        here = slice(b * KBLK, (b + 1) * KBLK)
        scores = lax.dot_general(query, ks_ref[here, :], NT, preferred_element_type=jnp.float32)
        block_top = jnp.max(scores, axis=1, keepdims=True)
        probs = jnp.exp2(scores * factor - block_top * factor).astype(jnp.bfloat16)
        part = jnp.dot(probs, vs_ref[here, :], preferred_element_type=jnp.float32)
        upper = jnp.maximum(top, block_top)
        acc = acc * jnp.exp2((top - upper) * factor) + part * jnp.exp2((block_top - upper) * factor)
        top = upper
    top = jnp.broadcast_to(top, (rows, LANES))

    lane = lax.broadcasted_iota(jnp.int32, (8, LANES), 1)
    for i, out_ref in enumerate(out_refs):
        start = i * block
        out_ref[:block, :] = acc[start : start + block, :width]
        stat = jnp.zeros((8, LANES), jnp.float32)
        for v in range(groups):
            at = slice(start + v * 8, start + v * 8 + 8)
            stat = jnp.where(lane == v, top[at, :], stat)
            stat = jnp.where(lane == groups + v, acc[at, width:], stat)
        out_ref[block:, :] = stat


def spread(stat, lane, width):
    return jnp.broadcast_to(stat[:, lane : lane + 1], (8, width))


def combine(refs, row, groups, width):
    rows = groups * 8
    g = row // 8
    stats = [ref[rows:, :] for ref in refs]
    tops = [spread(s, g, width) for s in stats]
    upper = functools.reduce(jnp.maximum, tops)
    out = jnp.zeros((8, width), jnp.float32)
    total = jnp.zeros((8, width), jnp.float32)
    for ref, s, t in zip(refs, stats, tops):
        weight = jnp.exp2((t - upper) * log2_scale(width))
        out = out + ref[row : row + 8, :] * weight
        total = total + spread(s, groups + g, width) * weight
    return out, upper, total


def pair_kernel(a_ref, b_ref, out_ref):
    rows, width = out_ref.shape
    rows = rows - STAT
    groups = rows // 8
    lane = lax.broadcasted_iota(jnp.int32, (8, LANES), 1)
    stat = jnp.zeros((8, LANES), jnp.float32)
    for g in range(groups):
        out, upper, total = combine((a_ref, b_ref), g * 8, groups, width)
        out_ref[g * 8 : g * 8 + 8, :] = out
        stat = jnp.where(lane == g, upper, stat)
        stat = jnp.where(lane == groups + g, total, stat)
    out_ref[rows:, :] = stat


def combine_kernel(a_ref, b_ref, c_ref, out_ref):
    peers, chunk_rows, width = out_ref.shape
    per = chunk_rows - STAT
    groups = peers * per // 8
    local = per // 8
    lane = lax.broadcasted_iota(jnp.int32, (8, LANES), 1)
    for p in range(peers):
        stat = jnp.zeros((8, LANES), jnp.float32)
        for v in range(local):
            out, upper, total = combine((a_ref, b_ref, c_ref), p * per + v * 8, groups, width)
            out_ref[p, v * 8 : v * 8 + 8, :] = out
            stat = jnp.where(lane == v, upper, stat)
            stat = jnp.where(lane == local + v, total, stat)
        out_ref[p, per:, :] = stat


def merge_kernel(in_ref, out_ref, row_ref):
    sources, chunk_rows, width = in_ref.shape
    copies = out_ref.shape[0]
    per = chunk_rows - STAT
    groups = per // 8
    factor = log2_scale(width)
    stat = in_ref[:, per:, :]
    for v in range(groups):
        tops = jnp.broadcast_to(stat[:, :, v : v + 1], (sources, 8, width))
        totals = jnp.broadcast_to(stat[:, :, groups + v : groups + v + 1], (sources, 8, width))
        upper = jnp.max(tops, axis=0)
        weight = jnp.exp2((tops - upper[None]) * factor)
        out = jnp.sum(in_ref[:, v * 8 : v * 8 + 8, :] * weight, axis=0)
        out = out / jnp.sum(totals * weight, axis=0)
        for g in range(8):
            row_ref[v : v + 1, g * width : (g + 1) * width] = out[g : g + 1, :]
    row = row_ref[...]
    for c in range(copies):
        out_ref[c] = row


def shards(queries, new_keys, new_values, cache_keys, cache_values, cache_lengths, offsets):
    heads = X * CORE
    rows, _, group, width = queries.shape
    per = rows * group
    positions = cache_keys.shape[1]
    vmem = pl.BlockSpec(memory_space=pltpu.VMEM)
    smem = pl.BlockSpec(memory_space=pltpu.SMEM)
    anywhere = pl.BlockSpec(memory_space=pl.ANY)
    params = pltpu.CompilerParams(vmem_limit_bytes=VMEM_LIMIT)
    place = jnp.stack([lax.axis_index("z"), lax.axis_index("y")]).astype(jnp.int32)

    def shift(block, distance):
        return lax.ppermute(block, "y", [(i, (i + distance) % Y) for i in range(Y)])

    with jax.named_scope("gather_queries"):
        mine = queries.reshape(per, width)
        every = lax.all_to_all(jnp.broadcast_to(mine[None], (Z * Y, per, width)), ("z", "y"), 0, 0)
        every = every.reshape(Z, Y, per, width)

    with jax.named_scope("prepare"):
        new = jnp.concatenate([new_keys[:, 0], new_values[:, 0]], axis=0)
        keys, values, visible = pl.pallas_call(
            prepare_kernel,
            out_shape=(
                jax.ShapeDtypeStruct((positions + LANES, width), cache_keys.dtype),
                jax.ShapeDtypeStruct((positions + LANES, 2 * width), cache_values.dtype),
                jax.ShapeDtypeStruct((Y, Z * rows, LANES), jnp.float32),
            ),
            in_specs=[smem] * 3 + [vmem] * 3,
            out_specs=[vmem] * 3,
            compiler_params=params,
        )(place, cache_lengths, offsets, cache_keys[0], cache_values[0], new)

    def attend(backs, *after):
        return pl.pallas_call(
            functools.partial(attend_kernel, backs),
            out_shape=[jax.ShapeDtypeStruct((Z * per + STAT, width), jnp.float32)] * len(backs),
            in_specs=[smem] + [vmem] * 4 + [anywhere] * len(after),
            out_specs=[vmem] * len(backs),
            compiler_params=params,
        )(place, every, keys, values, visible, *after)

    with jax.named_scope("attend_two_on"):
        (two_on,) = attend((2,))
        passing = shift(two_on, 1)
    with jax.named_scope("attend_neighbours"):
        behind, ahead = attend((1, 3), two_on)
    with jax.named_scope("pass_on"):
        ahead = pl.pallas_call(
            pair_kernel,
            out_shape=jax.ShapeDtypeStruct(ahead.shape, jnp.float32),
            in_specs=[vmem] * 2,
            out_specs=vmem,
            compiler_params=params,
        )(ahead, passing)
        from_behind, from_ahead = shift(ahead, 1), shift(behind, -1)
    with jax.named_scope("attend_own"):
        (own,) = attend((0,), ahead)

    with jax.named_scope("combine"):
        column = pl.pallas_call(
            combine_kernel,
            out_shape=jax.ShapeDtypeStruct((Z, per + STAT, width), jnp.float32),
            in_specs=[vmem] * 3,
            out_specs=vmem,
            compiler_params=params,
        )(own, from_behind, from_ahead)

    with jax.named_scope("exchange_z"):
        arrived = lax.all_to_all(column, "z", 0, 0)

    with jax.named_scope("merge"):
        merged = pl.pallas_call(
            merge_kernel,
            out_shape=jax.ShapeDtypeStruct((heads, rows, group * width), jnp.float32),
            in_specs=[vmem],
            out_specs=vmem,
            scratch_shapes=[pltpu.VMEM((rows, group * width), jnp.float32)],
            compiler_params=params,
        )(arrived)

    with jax.named_scope("gather_heads"):
        whole = lax.all_to_all(merged, ("x", "core"), 0, 0)
        return jnp.transpose(whole, (1, 0, 2)).reshape(rows, heads * group * width)


def solution(mesh):
    grid = Mesh(mesh.devices.reshape(Z, Y, X, CORE), ("z", "y", "x", "core"))
    ctx, kvh = ("z", "y"), ("x", "core")
    return jax.shard_map(
        shards,
        mesh=grid,
        in_specs=(
            P(ctx, kvh, None, None),
            P(ctx, kvh, None),
            P(ctx, kvh, None),
            P(kvh, ctx, None),
            P(kvh, ctx, None),
            P(ctx),
            P(),
        ),
        out_specs=P(ctx, None),
        check_vma=False,
    )
```

```python
import functools
import math

import jax
import jax.numpy as jnp
from jax import lax
from jax.experimental import pallas as pl
from jax.experimental.pallas import tpu as pltpu
from jax.sharding import Mesh
from jax.sharding import PartitionSpec as P

KBLK = 512
NEG = -1e30
LANES = 128
STAT = 8
NT = (((1,), (1,)), ((), ()))
Z, YH, YL, X, CORE = 8, 2, 2, 4, 2
Y = YH * YL
VMEM_LIMIT = 24 * 2**20


def log2_scale(width):
    return width**-0.5 * math.log2(math.e)


def prepare_kernel(place_ref, length_ref, offsets_ref, k_ref, v_ref, new_ref, ks_ref, vs_ref, vis_ref):
    positions, width = k_ref.shape
    fresh = new_ref.shape[0] // 2
    length = length_ref[0]
    ones = jnp.ones((KBLK, width), vs_ref.dtype)
    for b in range(positions // KBLK):
        here = slice(b * KBLK, (b + 1) * KBLK)

        @pl.when((b + 1) * KBLK <= length)
        def _():
            ks_ref[here, :] = k_ref[here, :]
            vs_ref[here, :width] = v_ref[here, :]
            vs_ref[here, width:] = ones

        @pl.when((b + 1) * KBLK > length)
        def _():
            inside = b * KBLK + lax.broadcasted_iota(jnp.int32, (KBLK, width), 0) < length
            first = k_ref[0:16, :].astype(jnp.float32)[0:1, :]
            keys = jnp.where(inside, k_ref[here, :].astype(jnp.float32), first)
            values = jnp.where(inside, v_ref[here, :].astype(jnp.float32), 0.0)
            ks_ref[here, :] = keys.astype(ks_ref.dtype)
            vs_ref[here, :width] = values.astype(vs_ref.dtype)
            vs_ref[here, width:] = jnp.where(inside, 1.0, 0.0).astype(vs_ref.dtype)

    row = lax.broadcasted_iota(jnp.int32, (LANES, width), 0)
    keys = jnp.zeros((LANES, width), jnp.float32)
    values = jnp.zeros((LANES, width), jnp.float32)
    new = new_ref[...].astype(jnp.float32)
    for j in range(2 * fresh):
        n = j % fresh
        keys = jnp.where(row == j, new[n : n + 1, :], keys)
        values = jnp.where(row == j, new[fresh + n : fresh + n + 1, :], values)
    ks_ref[positions : positions + LANES, :] = keys.astype(ks_ref.dtype)
    vs_ref[positions:, :width] = values.astype(vs_ref.dtype)
    vs_ref[positions:, width:] = jnp.where(row < 2 * fresh, 1.0, 0.0).astype(vs_ref.dtype)

    lane = lax.broadcasted_iota(jnp.int32, (1, LANES), 1)
    mine = jnp.full((1, LANES), 2**30, jnp.int32)
    start = (place_ref[0] * Y + place_ref[1]) * fresh
    for j in range(2 * fresh):
        mine = jnp.where(lane == j, offsets_ref[start + j % fresh], mine)
    for y in range(Y):
        for z in range(Z):
            for n in range(fresh):
                seen = mine <= offsets_ref[(z * Y + y) * fresh + n]
                at = (y * Z + z) * fresh + n
                vis_ref[at : at + 1, :] = jnp.where(seen, 1.0, 0.0)
    ks_ref[positions + LANES :, :] = vis_ref[...].astype(ks_ref.dtype)


def attend_kernel(backs, place_ref, q_ref, ks_ref, vs_ref, *refs):
    peers, _, per, width = q_ref.shape
    block = peers * per
    rows = block * len(backs)
    out_refs = refs[-len(backs) :]
    owners = [lax.rem(place_ref[1] + Y - back, Y) for back in backs]
    positions = vs_ref.shape[0] - LANES
    tokens = block // 8
    groups = block // 8
    factor = log2_scale(width)
    query = jnp.concatenate([q_ref[:, lax.div(owner, YL)].reshape(block, width) for owner in owners], axis=0)

    tops, parts = [], []
    for b in range(positions // KBLK):
        here = slice(b * KBLK, (b + 1) * KBLK)
        scores = lax.dot_general(query, ks_ref[here, :], NT, preferred_element_type=jnp.float32)
        top = jnp.max(scores, axis=1, keepdims=True)
        probs = jnp.exp2(scores * factor - top * factor).astype(jnp.bfloat16)
        tops.append(top)
        parts.append(jnp.dot(probs, vs_ref[here, :], preferred_element_type=jnp.float32))

    fresh = slice(positions, positions + LANES)
    scores = lax.dot_general(query, ks_ref[fresh, :], NT, preferred_element_type=jnp.float32)
    seen = [ks_ref[pl.ds(pl.multiple_of(fresh.stop + owner * tokens, tokens), tokens), :] for owner in owners]
    seen = jnp.concatenate([rows_seen.astype(jnp.float32) for rows_seen in seen], axis=0)
    seen = jnp.broadcast_to(seen[:, None, :], (rows // 8, 8, LANES)).reshape(rows, LANES) > 0
    scores = jnp.where(seen, scores, NEG)
    top = jnp.max(scores, axis=1, keepdims=True)
    probs = jnp.where(seen, jnp.exp2((scores - top) * factor), 0.0)
    rounded = probs.astype(jnp.bfloat16).astype(jnp.float32)
    lane = lax.broadcasted_iota(jnp.int32, (rows, LANES), 1)
    both = jnp.where(lane < 4, rounded, probs - rounded).astype(jnp.bfloat16)
    tops.append(top)
    parts.append(jnp.dot(both, vs_ref[fresh, :], preferred_element_type=jnp.float32))

    top = functools.reduce(jnp.maximum, tops)
    acc = functools.reduce(jnp.add, [part * jnp.exp2((t - top) * factor) for t, part in zip(tops, parts)])
    top = jnp.broadcast_to(top, (rows, LANES))

    lane = lax.broadcasted_iota(jnp.int32, (8, LANES), 1)
    for i, out_ref in enumerate(out_refs):
        start = i * block
        out_ref[:block, :] = acc[start : start + block, :width]
        stat = jnp.zeros((8, LANES), jnp.float32)
        for v in range(groups):
            at = slice(start + v * 8, start + v * 8 + 8)
            stat = jnp.where(lane == v, top[at, :], stat)
            stat = jnp.where(lane == groups + v, acc[at, width:], stat)
        out_ref[block:, :] = stat


def spread(stat, lane, width):
    return jnp.broadcast_to(stat[:, lane : lane + 1], (8, width))


def combine(refs, row, groups, width):
    rows = groups * 8
    g = row // 8
    stats = [ref[rows:, :] for ref in refs]
    tops = [spread(s, g, width) for s in stats]
    upper = functools.reduce(jnp.maximum, tops)
    out = jnp.zeros((8, width), jnp.float32)
    total = jnp.zeros((8, width), jnp.float32)
    for ref, s, t in zip(refs, stats, tops):
        weight = jnp.exp2((t - upper) * log2_scale(width))
        out = out + ref[row : row + 8, :] * weight
        total = total + spread(s, groups + g, width) * weight
    return out, upper, total


def pair_kernel(a_ref, b_ref, out_ref):
    rows, width = out_ref.shape
    rows = rows - STAT
    groups = rows // 8
    lane = lax.broadcasted_iota(jnp.int32, (8, LANES), 1)
    stat = jnp.zeros((8, LANES), jnp.float32)
    for g in range(groups):
        out, upper, total = combine((a_ref, b_ref), g * 8, groups, width)
        out_ref[g * 8 : g * 8 + 8, :] = out
        stat = jnp.where(lane == g, upper, stat)
        stat = jnp.where(lane == groups + g, total, stat)
    out_ref[rows:, :] = stat


def combine_kernel(a_ref, b_ref, c_ref, out_ref):
    peers, chunk_rows, width = out_ref.shape
    per = chunk_rows - STAT
    groups = peers * per // 8
    local = per // 8
    lane = lax.broadcasted_iota(jnp.int32, (8, LANES), 1)
    for p in range(peers):
        stat = jnp.zeros((8, LANES), jnp.float32)
        for v in range(local):
            out, upper, total = combine((a_ref, b_ref, c_ref), p * per + v * 8, groups, width)
            out_ref[p, v * 8 : v * 8 + 8, :] = out
            stat = jnp.where(lane == v, upper, stat)
            stat = jnp.where(lane == local + v, total, stat)
        out_ref[p, per:, :] = stat


def merge_kernel(in_ref, out_ref, row_ref):
    sources, chunk_rows, width = in_ref.shape
    copies = out_ref.shape[0]
    per = chunk_rows - STAT
    groups = per // 8
    factor = log2_scale(width)
    stat = in_ref[:, per:, :]
    for v in range(groups):
        tops = jnp.broadcast_to(stat[:, :, v : v + 1], (sources, 8, width))
        totals = jnp.broadcast_to(stat[:, :, groups + v : groups + v + 1], (sources, 8, width))
        upper = jnp.max(tops, axis=0)
        weight = jnp.exp2((tops - upper[None]) * factor)
        out = jnp.sum(in_ref[:, v * 8 : v * 8 + 8, :] * weight, axis=0)
        out = out / jnp.sum(totals * weight, axis=0)
        for g in range(8):
            row_ref[v : v + 1, g * width : (g + 1) * width] = out[g : g + 1, :]
    row = row_ref[...]
    for c in range(copies):
        out_ref[c] = row


def shards(queries, new_keys, new_values, cache_keys, cache_values, cache_lengths, offsets):
    heads = X * CORE
    rows, _, group, width = queries.shape
    per = rows * group
    positions = cache_keys.shape[1]
    vmem = pl.BlockSpec(memory_space=pltpu.VMEM)
    smem = pl.BlockSpec(memory_space=pltpu.SMEM)
    anywhere = pl.BlockSpec(memory_space=pl.ANY)
    params = pltpu.CompilerParams(vmem_limit_bytes=VMEM_LIMIT)
    ring = ("yh", "yl")
    place = jnp.stack([lax.axis_index("z"), lax.axis_index(ring)]).astype(jnp.int32)

    def shift(block, distance):
        return lax.ppermute(block, ring, [(i, (i + distance) % Y) for i in range(Y)])

    with jax.named_scope("gather_queries"):
        mine = queries.reshape(per, width)
        same = lax.all_to_all(jnp.broadcast_to(mine[None], (Z * YH, per, width)), ("z", "yh"), 0, 0)
        same = same.reshape(Z, YH, per, width)

    with jax.named_scope("prepare"):
        new = jnp.concatenate([new_keys[:, 0], new_values[:, 0]], axis=0)
        keys, values = pl.pallas_call(
            prepare_kernel,
            out_shape=(
                jax.ShapeDtypeStruct((positions + LANES + Z * Y * rows, width), cache_keys.dtype),
                jax.ShapeDtypeStruct((positions + LANES, 2 * width), cache_values.dtype),
            ),
            in_specs=[smem] * 3 + [vmem] * 3,
            out_specs=[vmem] * 2,
            scratch_shapes=[pltpu.VMEM((Z * Y * rows, LANES), jnp.float32)],
            compiler_params=params,
        )(place, cache_lengths, offsets, cache_keys[0], cache_values[0], new)

    with jax.named_scope("swap_parity"):
        same, keys, values = lax.optimization_barrier((same, keys, values))
        other = lax.ppermute(same, "yl", [(0, 1), (1, 0)])

    def attend(backs, rows_in, *after):
        return pl.pallas_call(
            functools.partial(attend_kernel, backs),
            out_shape=[jax.ShapeDtypeStruct((Z * per + STAT, width), jnp.float32)] * len(backs),
            in_specs=[smem] + [vmem] * 3 + [anywhere] * len(after),
            out_specs=[vmem] * len(backs),
            compiler_params=params,
            cost_estimate=pl.CostEstimate(
                flops=4 * len(backs) * Z * per * positions * 4 * width,
                transcendentals=len(backs) * Z * per * positions,
                bytes_accessed=8 * positions * width,
            ),
        )(place, rows_in, keys, values, *after)

    with jax.named_scope("attend_two_on"):
        (two_on,) = attend((2,), same)
        passing = shift(two_on, 1)
    with jax.named_scope("attend_neighbours"):
        behind, ahead = attend((1, 3), other, two_on)
    with jax.named_scope("pass_on"):
        ahead = pl.pallas_call(
            pair_kernel,
            out_shape=jax.ShapeDtypeStruct(ahead.shape, jnp.float32),
            in_specs=[vmem] * 2,
            out_specs=vmem,
            compiler_params=params,
        )(ahead, passing)
        from_behind, from_ahead = shift(ahead, 1), shift(behind, -1)
    with jax.named_scope("attend_own"):
        (own,) = attend((0,), same, ahead)

    with jax.named_scope("combine"):
        column = pl.pallas_call(
            combine_kernel,
            out_shape=jax.ShapeDtypeStruct((Z, per + STAT, width), jnp.float32),
            in_specs=[vmem] * 3,
            out_specs=vmem,
            compiler_params=params,
        )(own, from_behind, from_ahead)

    with jax.named_scope("exchange_z"):
        arrived = lax.all_to_all(column, "z", 0, 0)

    with jax.named_scope("merge"):
        merged = pl.pallas_call(
            merge_kernel,
            out_shape=jax.ShapeDtypeStruct((heads, rows, group * width), jnp.float32),
            in_specs=[vmem],
            out_specs=vmem,
            scratch_shapes=[pltpu.VMEM((rows, group * width), jnp.float32)],
            compiler_params=params,
        )(arrived)

    with jax.named_scope("gather_heads"):
        whole = lax.all_to_all(merged, ("x", "core"), 0, 0)
        return jnp.transpose(whole, (1, 0, 2)).reshape(rows, heads * group * width)


def solution(mesh):
    grid = Mesh(mesh.devices.reshape(Z, YH, YL, X, CORE), ("z", "yh", "yl", "x", "core"))
    ctx, kvh = ("z", "yh", "yl"), ("x", "core")
    return jax.shard_map(
        shards,
        mesh=grid,
        in_specs=(
            P(ctx, kvh, None, None),
            P(ctx, kvh, None),
            P(ctx, kvh, None),
            P(kvh, ctx, None),
            P(kvh, ctx, None),
            P(ctx),
            P(),
        ),
        out_specs=P(ctx, None),
        check_vma=False,
    )
```

```python
import functools
import math

import jax
import jax.numpy as jnp
from jax import lax
from jax.experimental import pallas as pl
from jax.experimental.pallas import tpu as pltpu
from jax.sharding import Mesh
from jax.sharding import PartitionSpec as P

KBLK = 512
NEG = -1e30
LANES = 128
STAT = 8
NT = (((1,), (1,)), ((), ()))
Z, YH, YL, X, CORE = 8, 2, 2, 4, 2
Y = YH * YL
VMEM_LIMIT = 24 * 2**20


def log2_scale(width):
    return width**-0.5 * math.log2(math.e)


def prepare_kernel(place_ref, length_ref, offsets_ref, k_ref, v_ref, new_ref, ks_ref, vs_ref, vis_ref):
    positions, width = k_ref.shape
    fresh = new_ref.shape[0] // 2
    length = length_ref[0]
    ones = jnp.ones((KBLK, width), vs_ref.dtype)
    for b in range(positions // KBLK):
        here = slice(b * KBLK, (b + 1) * KBLK)

        @pl.when((b + 1) * KBLK <= length)
        def _():
            ks_ref[here, :] = k_ref[here, :]
            vs_ref[here, :width] = v_ref[here, :]
            vs_ref[here, width:] = ones

        @pl.when((b + 1) * KBLK > length)
        def _():
            inside = b * KBLK + lax.broadcasted_iota(jnp.int32, (KBLK, width), 0) < length
            first = k_ref[0:16, :].astype(jnp.float32)[0:1, :]
            keys = jnp.where(inside, k_ref[here, :].astype(jnp.float32), first)
            values = jnp.where(inside, v_ref[here, :].astype(jnp.float32), 0.0)
            ks_ref[here, :] = keys.astype(ks_ref.dtype)
            vs_ref[here, :width] = values.astype(vs_ref.dtype)
            vs_ref[here, width:] = jnp.where(inside, 1.0, 0.0).astype(vs_ref.dtype)

    row = lax.broadcasted_iota(jnp.int32, (LANES, width), 0)
    keys = jnp.zeros((LANES, width), jnp.float32)
    values = jnp.zeros((LANES, width), jnp.float32)
    new = new_ref[...].astype(jnp.float32)
    for j in range(2 * fresh):
        n = j % fresh
        keys = jnp.where(row == j, new[n : n + 1, :], keys)
        values = jnp.where(row == j, new[fresh + n : fresh + n + 1, :], values)
    ks_ref[positions : positions + LANES, :] = keys.astype(ks_ref.dtype)
    vs_ref[positions:, :width] = values.astype(vs_ref.dtype)
    vs_ref[positions:, width:] = jnp.where(row < 2 * fresh, 1.0, 0.0).astype(vs_ref.dtype)

    lane = lax.broadcasted_iota(jnp.int32, (1, LANES), 1)
    mine = jnp.full((1, LANES), 2**30, jnp.int32)
    start = (place_ref[0] * Y + place_ref[1]) * fresh
    for j in range(2 * fresh):
        mine = jnp.where(lane == j, offsets_ref[start + j % fresh], mine)
    for y in range(Y):
        for z in range(Z):
            for n in range(fresh):
                seen = mine <= offsets_ref[(z * Y + y) * fresh + n]
                at = (y * Z + z) * fresh + n
                vis_ref[at : at + 1, :] = jnp.where(seen, 1.0, 0.0)
    ks_ref[positions + LANES :, :] = vis_ref[...].astype(ks_ref.dtype)


def attend_kernel(backs, place_ref, q_ref, ks_ref, vs_ref, *refs):
    peers, _, per, width = q_ref.shape
    block = peers * per
    rows = block * len(backs)
    out_refs = refs[-len(backs) :]
    owners = [lax.rem(place_ref[1] + Y - back, Y) for back in backs]
    positions = vs_ref.shape[0] - LANES
    tokens = block // 8
    groups = block // 8
    factor = log2_scale(width)
    query = jnp.concatenate([q_ref[:, lax.div(owner, YL)].reshape(block, width) for owner in owners], axis=0)

    tops, parts = [], []
    for b in range(positions // KBLK):
        here = slice(b * KBLK, (b + 1) * KBLK)
        scores = lax.dot_general(query, ks_ref[here, :], NT, preferred_element_type=jnp.float32)
        top = jnp.max(scores, axis=1, keepdims=True)
        probs = jnp.exp2(scores * factor - top * factor).astype(jnp.bfloat16)
        tops.append(top)
        parts.append(jnp.dot(probs, vs_ref[here, :], preferred_element_type=jnp.float32))

    fresh = slice(positions, positions + LANES)
    scores = lax.dot_general(query, ks_ref[fresh, :], NT, preferred_element_type=jnp.float32)
    seen = [ks_ref[pl.ds(pl.multiple_of(fresh.stop + owner * tokens, tokens), tokens), :] for owner in owners]
    seen = jnp.concatenate([rows_seen.astype(jnp.float32) for rows_seen in seen], axis=0)
    seen = jnp.broadcast_to(seen[:, None, :], (rows // 8, 8, LANES)).reshape(rows, LANES) > 0
    scores = jnp.where(seen, scores, NEG)
    top = jnp.max(scores, axis=1, keepdims=True)
    probs = jnp.where(seen, jnp.exp2((scores - top) * factor), 0.0)
    rounded = probs.astype(jnp.bfloat16).astype(jnp.float32)
    lane = lax.broadcasted_iota(jnp.int32, (rows, LANES), 1)
    both = jnp.where(lane < 4, rounded, probs - rounded).astype(jnp.bfloat16)
    tops.append(top)
    parts.append(jnp.dot(both, vs_ref[fresh, :], preferred_element_type=jnp.float32))

    top = functools.reduce(jnp.maximum, tops)
    acc = functools.reduce(jnp.add, [part * jnp.exp2((t - top) * factor) for t, part in zip(tops, parts)])
    top = jnp.broadcast_to(top, (rows, LANES))

    lane = lax.broadcasted_iota(jnp.int32, (8, LANES), 1)
    for i, out_ref in enumerate(out_refs):
        start = i * block
        out_ref[:block, :] = acc[start : start + block, :width]
        stat = jnp.zeros((8, LANES), jnp.float32)
        for v in range(groups):
            at = slice(start + v * 8, start + v * 8 + 8)
            stat = jnp.where(lane == v, top[at, :], stat)
            stat = jnp.where(lane == groups + v, acc[at, width:], stat)
        out_ref[block:, :] = stat


def spread(stat, lane, width):
    return jnp.broadcast_to(stat[:, lane : lane + 1], (8, width))


def combine(refs, row, groups, width):
    rows = groups * 8
    g = row // 8
    stats = [ref[rows:, :] for ref in refs]
    tops = [spread(s, g, width) for s in stats]
    upper = functools.reduce(jnp.maximum, tops)
    out = jnp.zeros((8, width), jnp.float32)
    total = jnp.zeros((8, width), jnp.float32)
    for ref, s, t in zip(refs, stats, tops):
        weight = jnp.exp2((t - upper) * log2_scale(width))
        out = out + ref[row : row + 8, :] * weight
        total = total + spread(s, groups + g, width) * weight
    return out, upper, total


def pair_kernel(a_ref, b_ref, out_ref):
    rows, width = out_ref.shape
    rows = rows - STAT
    groups = rows // 8
    lane = lax.broadcasted_iota(jnp.int32, (8, LANES), 1)
    stat = jnp.zeros((8, LANES), jnp.float32)
    for g in range(groups):
        out, upper, total = combine((a_ref, b_ref), g * 8, groups, width)
        out_ref[g * 8 : g * 8 + 8, :] = out
        stat = jnp.where(lane == g, upper, stat)
        stat = jnp.where(lane == groups + g, total, stat)
    out_ref[rows:, :] = stat


def combine_kernel(a_ref, b_ref, c_ref, out_ref):
    peers, chunk_rows, width = out_ref.shape
    per = chunk_rows - STAT
    groups = peers * per // 8
    local = per // 8
    lane = lax.broadcasted_iota(jnp.int32, (8, LANES), 1)
    for p in range(peers):
        stat = jnp.zeros((8, LANES), jnp.float32)
        for v in range(local):
            out, upper, total = combine((a_ref, b_ref, c_ref), p * per + v * 8, groups, width)
            out_ref[p, v * 8 : v * 8 + 8, :] = out
            stat = jnp.where(lane == v, upper, stat)
            stat = jnp.where(lane == local + v, total, stat)
        out_ref[p, per:, :] = stat


def merge_kernel(in_ref, out_ref, row_ref):
    sources, chunk_rows, width = in_ref.shape
    per = chunk_rows - STAT
    groups = per // 8
    factor = log2_scale(width)
    stat = in_ref[:, per:, :]
    for v in range(groups):
        tops = jnp.broadcast_to(stat[:, :, v : v + 1], (sources, 8, width))
        totals = jnp.broadcast_to(stat[:, :, groups + v : groups + v + 1], (sources, 8, width))
        upper = jnp.max(tops, axis=0)
        weight = jnp.exp2((tops - upper[None]) * factor)
        out = jnp.sum(in_ref[:, v * 8 : v * 8 + 8, :] * weight, axis=0)
        out = out / jnp.sum(totals * weight, axis=0)
        for g in range(8):
            row_ref[v : v + 1, g * width : (g + 1) * width] = out[g : g + 1, :]
    row = row_ref[...]
    for c in range(out_ref.shape[1] // row.shape[1]):
        out_ref[:, c * row.shape[1] : (c + 1) * row.shape[1]] = row


def shards(queries, new_keys, new_values, cache_keys, cache_values, cache_lengths, offsets):
    heads = X * CORE
    rows, _, group, width = queries.shape
    per = rows * group
    positions = cache_keys.shape[1]
    vmem = pl.BlockSpec(memory_space=pltpu.VMEM)
    smem = pl.BlockSpec(memory_space=pltpu.SMEM)
    anywhere = pl.BlockSpec(memory_space=pl.ANY)
    params = pltpu.CompilerParams(vmem_limit_bytes=VMEM_LIMIT)
    ring = ("yh", "yl")
    place = jnp.stack([lax.axis_index("z"), lax.axis_index(ring)]).astype(jnp.int32)

    def shift(block, distance):
        return lax.ppermute(block, ring, [(i, (i + distance) % Y) for i in range(Y)])

    with jax.named_scope("gather_queries"):
        mine = queries.reshape(per, width)
        same = lax.all_to_all(jnp.broadcast_to(mine[None], (Z * YH, per, width)), ("z", "yh"), 0, 0)
        same = same.reshape(Z, YH, per, width)

    with jax.named_scope("prepare"):
        new = jnp.concatenate([new_keys[:, 0], new_values[:, 0]], axis=0)
        keys, values = pl.pallas_call(
            prepare_kernel,
            out_shape=(
                jax.ShapeDtypeStruct((positions + LANES + Z * Y * rows, width), cache_keys.dtype),
                jax.ShapeDtypeStruct((positions + LANES, 2 * width), cache_values.dtype),
            ),
            in_specs=[smem] * 3 + [vmem] * 3,
            out_specs=[vmem] * 2,
            scratch_shapes=[pltpu.VMEM((Z * Y * rows, LANES), jnp.float32)],
            compiler_params=params,
        )(place, cache_lengths, offsets, cache_keys[0], cache_values[0], new)

    with jax.named_scope("swap_parity"):
        same, keys, values = lax.optimization_barrier((same, keys, values))
        other = lax.ppermute(same, "yl", [(0, 1), (1, 0)])

    def attend(backs, rows_in, *after):
        return pl.pallas_call(
            functools.partial(attend_kernel, backs),
            out_shape=[jax.ShapeDtypeStruct((Z * per + STAT, width), jnp.float32)] * len(backs),
            in_specs=[smem] + [vmem] * 3 + [anywhere] * len(after),
            out_specs=[vmem] * len(backs),
            compiler_params=params,
            cost_estimate=pl.CostEstimate(
                flops=4 * len(backs) * Z * per * positions * 4 * width,
                transcendentals=len(backs) * Z * per * positions,
                bytes_accessed=8 * positions * width,
            ),
        )(place, rows_in, keys, values, *after)

    with jax.named_scope("attend_two_on"):
        (two_on,) = attend((2,), same)
        passing = shift(two_on, 1)
    with jax.named_scope("attend_neighbours"):
        behind, ahead = attend((1, 3), other, two_on)
    with jax.named_scope("pass_on"):
        ahead = pl.pallas_call(
            pair_kernel,
            out_shape=jax.ShapeDtypeStruct(ahead.shape, jnp.float32),
            in_specs=[vmem] * 2,
            out_specs=vmem,
            compiler_params=params,
        )(ahead, passing)
        from_behind = shift(ahead, 1)
        behind, _ = lax.optimization_barrier((behind, ahead))
        from_ahead = shift(behind, -1)
    with jax.named_scope("attend_own"):
        (own,) = attend((0,), same, ahead)

    with jax.named_scope("combine"):
        column = pl.pallas_call(
            combine_kernel,
            out_shape=jax.ShapeDtypeStruct((Z, per + STAT, width), jnp.float32),
            in_specs=[vmem] * 3,
            out_specs=vmem,
            compiler_params=params,
        )(own, from_behind, from_ahead)

    with jax.named_scope("exchange_z"):
        arrived = lax.all_to_all(column, "z", 0, 0)

    with jax.named_scope("merge"):
        merged = pl.pallas_call(
            merge_kernel,
            out_shape=jax.ShapeDtypeStruct((rows, heads * group * width), jnp.float32),
            in_specs=[vmem],
            out_specs=vmem,
            scratch_shapes=[pltpu.VMEM((rows, group * width), jnp.float32)],
            compiler_params=params,
        )(arrived)

    with jax.named_scope("gather_heads"):
        return lax.all_to_all(merged, ("x", "core"), 1, 1, tiled=True)


def solution(mesh):
    grid = Mesh(mesh.devices.reshape(Z, YH, YL, X, CORE), ("z", "yh", "yl", "x", "core"))
    ctx, kvh = ("z", "yh", "yl"), ("x", "core")
    return jax.shard_map(
        shards,
        mesh=grid,
        in_specs=(
            P(ctx, kvh, None, None),
            P(ctx, kvh, None),
            P(ctx, kvh, None),
            P(kvh, ctx, None),
            P(kvh, ctx, None),
            P(ctx),
            P(),
        ),
        out_specs=P(ctx, None),
        check_vma=False,
    )
```

```python
import functools
import math

import jax
import jax.numpy as jnp
from jax import lax
from jax.experimental import pallas as pl
from jax.experimental.pallas import tpu as pltpu
from jax.sharding import Mesh
from jax.sharding import PartitionSpec as P

KBLK = 512
NEG = -1e30
LANES = 128
STAT = 8
NT = (((1,), (1,)), ((), ()))
Z, YH, YL, X, CORE = 8, 2, 2, 4, 2
Y = YH * YL
Z_FIRST, YH_FIRST = 4, 1
Z_MERGE = 5
HEAD_FIRST = 5
VMEM_LIMIT = 24 * 2**20


def z_at(i):
    return (i + Z_FIRST) % Z


def log2_scale(width):
    return width**-0.5 * math.log2(math.e)


def prepare_kernel(place_ref, length_ref, offsets_ref, k_ref, v_ref, new_ref, ks_ref, vs_ref, vis_ref):
    positions, width = k_ref.shape
    fresh = new_ref.shape[0] // 2
    length = length_ref[0]
    ones = jnp.ones((KBLK, width), vs_ref.dtype)
    for b in range(positions // KBLK):
        here = slice(b * KBLK, (b + 1) * KBLK)

        @pl.when((b + 1) * KBLK <= length)
        def _():
            ks_ref[here, :] = k_ref[here, :]
            vs_ref[here, :width] = v_ref[here, :]
            vs_ref[here, width:] = ones

        @pl.when((b + 1) * KBLK > length)
        def _():
            inside = b * KBLK + lax.broadcasted_iota(jnp.int32, (KBLK, width), 0) < length
            first = k_ref[0:16, :].astype(jnp.float32)[0:1, :]
            keys = jnp.where(inside, k_ref[here, :].astype(jnp.float32), first)
            values = jnp.where(inside, v_ref[here, :].astype(jnp.float32), 0.0)
            ks_ref[here, :] = keys.astype(ks_ref.dtype)
            vs_ref[here, :width] = values.astype(vs_ref.dtype)
            vs_ref[here, width:] = jnp.where(inside, 1.0, 0.0).astype(vs_ref.dtype)

    row = lax.broadcasted_iota(jnp.int32, (LANES, width), 0)
    keys = jnp.zeros((LANES, width), jnp.float32)
    values = jnp.zeros((LANES, width), jnp.float32)
    new = new_ref[...].astype(jnp.float32)
    for j in range(2 * fresh):
        n = j % fresh
        keys = jnp.where(row == j, new[n : n + 1, :], keys)
        values = jnp.where(row == j, new[fresh + n : fresh + n + 1, :], values)
    ks_ref[positions : positions + LANES, :] = keys.astype(ks_ref.dtype)
    vs_ref[positions:, :width] = values.astype(vs_ref.dtype)
    vs_ref[positions:, width:] = jnp.where(row < 2 * fresh, 1.0, 0.0).astype(vs_ref.dtype)

    lane = lax.broadcasted_iota(jnp.int32, (1, LANES), 1)
    mine = jnp.full((1, LANES), 2**30, jnp.int32)
    start = (place_ref[0] * Y + place_ref[1]) * fresh
    for j in range(2 * fresh):
        mine = jnp.where(lane == j, offsets_ref[start + j % fresh], mine)
    for y in range(Y):
        for z in range(Z):
            for n in range(fresh):
                seen = mine <= offsets_ref[(z_at(z) * Y + y) * fresh + n]
                at = (y * Z + z) * fresh + n
                vis_ref[at : at + 1, :] = jnp.where(seen, 1.0, 0.0)
    ks_ref[positions + LANES :, :] = vis_ref[...].astype(ks_ref.dtype)


def attend_kernel(backs, place_ref, q_ref, ks_ref, vs_ref, *refs):
    peers, _, per, width = q_ref.shape
    block = peers * per
    rows = block * len(backs)
    out_refs = refs[-len(backs) :]
    owners = [lax.rem(place_ref[1] + Y - back, Y) for back in backs]
    positions = vs_ref.shape[0] - LANES
    tokens = block // 8
    groups = block // 8
    factor = log2_scale(width)
    query = jnp.concatenate([q_ref[:, lax.rem(lax.div(owner, YL) + YH - YH_FIRST, YH)].reshape(block, width) for owner in owners], axis=0)

    tops, parts = [], []
    for b in range(positions // KBLK):
        here = slice(b * KBLK, (b + 1) * KBLK)
        scores = lax.dot_general(query, ks_ref[here, :], NT, preferred_element_type=jnp.float32)
        top = jnp.max(scores, axis=1, keepdims=True)
        probs = jnp.exp2(scores * factor - top * factor).astype(jnp.bfloat16)
        tops.append(top)
        parts.append(jnp.dot(probs, vs_ref[here, :], preferred_element_type=jnp.float32))

    fresh = slice(positions, positions + LANES)
    scores = lax.dot_general(query, ks_ref[fresh, :], NT, preferred_element_type=jnp.float32)
    seen = [ks_ref[pl.ds(pl.multiple_of(fresh.stop + owner * tokens, tokens), tokens), :] for owner in owners]
    seen = jnp.concatenate([rows_seen.astype(jnp.float32) for rows_seen in seen], axis=0)
    seen = jnp.broadcast_to(seen[:, None, :], (rows // 8, 8, LANES)).reshape(rows, LANES) > 0
    scores = jnp.where(seen, scores, NEG)
    top = jnp.max(scores, axis=1, keepdims=True)
    probs = jnp.where(seen, jnp.exp2((scores - top) * factor), 0.0)
    rounded = probs.astype(jnp.bfloat16).astype(jnp.float32)
    lane = lax.broadcasted_iota(jnp.int32, (rows, LANES), 1)
    both = jnp.where(lane < 4, rounded, probs - rounded).astype(jnp.bfloat16)
    tops.append(top)
    parts.append(jnp.dot(both, vs_ref[fresh, :], preferred_element_type=jnp.float32))

    top = functools.reduce(jnp.maximum, tops)
    acc = functools.reduce(jnp.add, [part * jnp.exp2((t - top) * factor) for t, part in zip(tops, parts)])
    top = jnp.broadcast_to(top, (rows, LANES))

    lane = lax.broadcasted_iota(jnp.int32, (8, LANES), 1)
    for i, out_ref in enumerate(out_refs):
        start = i * block
        out_ref[:block, :] = acc[start : start + block, :width]
        stat = jnp.zeros((8, LANES), jnp.float32)
        for v in range(groups):
            at = slice(start + v * 8, start + v * 8 + 8)
            stat = jnp.where(lane == v, top[at, :], stat)
            stat = jnp.where(lane == groups + v, acc[at, width:], stat)
        out_ref[block:, :] = stat


def spread(stat, lane, width):
    return jnp.broadcast_to(stat[:, lane : lane + 1], (8, width))


def combine(refs, row, groups, width):
    rows = groups * 8
    g = row // 8
    stats = [ref[rows:, :] for ref in refs]
    tops = [spread(s, g, width) for s in stats]
    upper = functools.reduce(jnp.maximum, tops)
    out = jnp.zeros((8, width), jnp.float32)
    total = jnp.zeros((8, width), jnp.float32)
    for ref, s, t in zip(refs, stats, tops):
        weight = jnp.exp2((t - upper) * log2_scale(width))
        out = out + ref[row : row + 8, :] * weight
        total = total + spread(s, groups + g, width) * weight
    return out, upper, total


def pair_kernel(a_ref, b_ref, out_ref):
    rows, width = out_ref.shape
    rows = rows - STAT
    groups = rows // 8
    lane = lax.broadcasted_iota(jnp.int32, (8, LANES), 1)
    stat = jnp.zeros((8, LANES), jnp.float32)
    for g in range(groups):
        out, upper, total = combine((a_ref, b_ref), g * 8, groups, width)
        out_ref[g * 8 : g * 8 + 8, :] = out
        stat = jnp.where(lane == g, upper, stat)
        stat = jnp.where(lane == groups + g, total, stat)
    out_ref[rows:, :] = stat


def combine_kernel(a_ref, b_ref, c_ref, out_ref):
    peers, chunk_rows, width = out_ref.shape
    per = chunk_rows - STAT
    groups = peers * per // 8
    local = per // 8
    lane = lax.broadcasted_iota(jnp.int32, (8, LANES), 1)
    for p in range(peers):
        stat = jnp.zeros((8, LANES), jnp.float32)
        place = (p + Z_MERGE - Z_FIRST) % Z
        for v in range(local):
            out, upper, total = combine((a_ref, b_ref, c_ref), place * per + v * 8, groups, width)
            out_ref[p, v * 8 : v * 8 + 8, :] = out
            stat = jnp.where(lane == v, upper, stat)
            stat = jnp.where(lane == local + v, total, stat)
        out_ref[p, per:, :] = stat


def merge_kernel(in_ref, out_ref, row_ref):
    sources, chunk_rows, width = in_ref.shape
    per = chunk_rows - STAT
    groups = per // 8
    factor = log2_scale(width)
    stat = in_ref[:, per:, :]
    for v in range(groups):
        tops = jnp.broadcast_to(stat[:, :, v : v + 1], (sources, 8, width))
        totals = jnp.broadcast_to(stat[:, :, groups + v : groups + v + 1], (sources, 8, width))
        upper = jnp.max(tops, axis=0)
        weight = jnp.exp2((tops - upper[None]) * factor)
        out = jnp.sum(in_ref[:, v * 8 : v * 8 + 8, :] * weight, axis=0)
        out = out / jnp.sum(totals * weight, axis=0)
        for g in range(8):
            row_ref[v : v + 1, g * width : (g + 1) * width] = out[g : g + 1, :]
    row = row_ref[...]
    for c in range(out_ref.shape[1] // row.shape[1]):
        out_ref[:, c * row.shape[1] : (c + 1) * row.shape[1]] = row


def shards(queries, new_keys, new_values, cache_keys, cache_values, cache_lengths, offsets):
    heads = X * CORE
    rows, _, group, width = queries.shape
    per = rows * group
    positions = cache_keys.shape[1]
    vmem = pl.BlockSpec(memory_space=pltpu.VMEM)
    smem = pl.BlockSpec(memory_space=pltpu.SMEM)
    anywhere = pl.BlockSpec(memory_space=pl.ANY)
    params = pltpu.CompilerParams(vmem_limit_bytes=VMEM_LIMIT)
    ring = ("yh", "yl")
    place = jnp.stack([lax.axis_index("z"), lax.axis_index(ring)]).astype(jnp.int32)

    def shift(block, distance):
        return lax.ppermute(block, ring, [(i, (i + distance) % Y) for i in range(Y)])

    with jax.named_scope("gather_queries"):
        mine = queries.reshape(per, width)
        order = [[z_at(i) * YH + (yh + YH_FIRST) % YH for i in range(Z) for yh in range(YH)]]
        copies = jnp.broadcast_to(mine[None], (Z * YH, per, width))
        same = lax.all_to_all(copies, ("z", "yh"), 0, 0, axis_index_groups=order)
        same = same.reshape(Z, YH, per, width)

    with jax.named_scope("prepare"):
        new = jnp.concatenate([new_keys[:, 0], new_values[:, 0]], axis=0)
        keys, values = pl.pallas_call(
            prepare_kernel,
            out_shape=(
                jax.ShapeDtypeStruct((positions + LANES + Z * Y * rows, width), cache_keys.dtype),
                jax.ShapeDtypeStruct((positions + LANES, 2 * width), cache_values.dtype),
            ),
            in_specs=[smem] * 3 + [vmem] * 3,
            out_specs=[vmem] * 2,
            scratch_shapes=[pltpu.VMEM((Z * Y * rows, LANES), jnp.float32)],
            compiler_params=params,
        )(place, cache_lengths, offsets, cache_keys[0], cache_values[0], new)

    with jax.named_scope("swap_parity"):
        same, keys, values = lax.optimization_barrier((same, keys, values))
        other = lax.ppermute(same, "yl", [(0, 1), (1, 0)])

    def attend(backs, rows_in, *after):
        return pl.pallas_call(
            functools.partial(attend_kernel, backs),
            out_shape=[jax.ShapeDtypeStruct((Z * per + STAT, width), jnp.float32)] * len(backs),
            in_specs=[smem] + [vmem] * 3 + [anywhere] * len(after),
            out_specs=[vmem] * len(backs),
            compiler_params=params,
            cost_estimate=pl.CostEstimate(
                flops=4 * len(backs) * Z * per * positions * 4 * width,
                transcendentals=len(backs) * Z * per * positions,
                bytes_accessed=8 * positions * width,
            ),
        )(place, rows_in, keys, values, *after)

    with jax.named_scope("attend_two_on"):
        (two_on,) = attend((2,), same)
        passing = shift(two_on, 1)
    with jax.named_scope("attend_neighbours"):
        behind, ahead = attend((1, 3), other, two_on)
    with jax.named_scope("pass_on"):
        ahead = pl.pallas_call(
            pair_kernel,
            out_shape=jax.ShapeDtypeStruct(ahead.shape, jnp.float32),
            in_specs=[vmem] * 2,
            out_specs=vmem,
            compiler_params=params,
        )(ahead, passing)
        from_behind = shift(ahead, 1)
        behind, _ = lax.optimization_barrier((behind, ahead))
        from_ahead = shift(behind, -1)
    with jax.named_scope("attend_own"):
        (own,) = attend((0,), same, ahead)

    with jax.named_scope("combine"):
        column = pl.pallas_call(
            combine_kernel,
            out_shape=jax.ShapeDtypeStruct((Z, per + STAT, width), jnp.float32),
            in_specs=[vmem] * 3,
            out_specs=vmem,
            compiler_params=params,
        )(own, from_behind, from_ahead)

    with jax.named_scope("exchange_z"):
        order = [[(i + Z_MERGE) % Z for i in range(Z)]]
        arrived = lax.all_to_all(column, "z", 0, 0, axis_index_groups=order)

    with jax.named_scope("merge"):
        merged = pl.pallas_call(
            merge_kernel,
            out_shape=jax.ShapeDtypeStruct((rows, heads * group * width), jnp.float32),
            in_specs=[vmem],
            out_specs=vmem,
            scratch_shapes=[pltpu.VMEM((rows, group * width), jnp.float32)],
            compiler_params=params,
        )(arrived)

    with jax.named_scope("gather_heads"):
        order = [[(i + HEAD_FIRST) % heads for i in range(heads)]]
        whole = lax.all_to_all(merged, ("x", "core"), 1, 1, tiled=True, axis_index_groups=order)
        return jnp.roll(whole, HEAD_FIRST * group * width, axis=1)


def solution(mesh):
    grid = Mesh(mesh.devices.reshape(Z, YH, YL, X, CORE), ("z", "yh", "yl", "x", "core"))
    ctx, kvh = ("z", "yh", "yl"), ("x", "core")
    return jax.shard_map(
        shards,
        mesh=grid,
        in_specs=(
            P(ctx, kvh, None, None),
            P(ctx, kvh, None),
            P(ctx, kvh, None),
            P(kvh, ctx, None),
            P(kvh, ctx, None),
            P(ctx),
            P(),
        ),
        out_specs=P(ctx, None),
        check_vma=False,
    )
```

```python
import functools
import math

import jax
import jax.numpy as jnp
from jax import lax
from jax.experimental import pallas as pl
from jax.experimental.pallas import tpu as pltpu
from jax.sharding import Mesh
from jax.sharding import PartitionSpec as P

KBLK = 512
NEG = -1e30
LANES = 128
STAT = 8
NT = (((1,), (1,)), ((), ()))
Z, YH, YL, X, CORE = 8, 2, 2, 4, 2
Y = YH * YL
Z_FIRST, YH_FIRST = 5, 1
Z_MERGE = 5
HEAD_FIRST = 5
OWN, ACROSS, OPPOSITE, BESIDE = range(4)
VMEM_LIMIT = 24 * 2**20


def z_at(i):
    return (i + Z_FIRST) % Z


def log2_scale(width):
    return width**-0.5 * math.log2(math.e)


def prepare_kernel(place_ref, length_ref, offsets_ref, k_ref, v_ref, new_ref, ks_ref, vs_ref, vis_ref):
    positions, width = k_ref.shape
    fresh = new_ref.shape[0] // 2
    length = length_ref[0]
    ones = jnp.ones((KBLK, width), vs_ref.dtype)
    for b in range(positions // KBLK):
        here = slice(b * KBLK, (b + 1) * KBLK)

        @pl.when((b + 1) * KBLK <= length)
        def _():
            ks_ref[here, :] = k_ref[here, :]
            vs_ref[here, :width] = v_ref[here, :]
            vs_ref[here, width:] = ones

        @pl.when((b + 1) * KBLK > length)
        def _():
            inside = b * KBLK + lax.broadcasted_iota(jnp.int32, (KBLK, width), 0) < length
            first = k_ref[0:16, :].astype(jnp.float32)[0:1, :]
            keys = jnp.where(inside, k_ref[here, :].astype(jnp.float32), first)
            values = jnp.where(inside, v_ref[here, :].astype(jnp.float32), 0.0)
            ks_ref[here, :] = keys.astype(ks_ref.dtype)
            vs_ref[here, :width] = values.astype(vs_ref.dtype)
            vs_ref[here, width:] = jnp.where(inside, 1.0, 0.0).astype(vs_ref.dtype)

    row = lax.broadcasted_iota(jnp.int32, (LANES, width), 0)
    keys = jnp.zeros((LANES, width), jnp.float32)
    values = jnp.zeros((LANES, width), jnp.float32)
    new = new_ref[...].astype(jnp.float32)
    for j in range(2 * fresh):
        n = j % fresh
        keys = jnp.where(row == j, new[n : n + 1, :], keys)
        values = jnp.where(row == j, new[fresh + n : fresh + n + 1, :], values)
    ks_ref[positions : positions + LANES, :] = keys.astype(ks_ref.dtype)
    vs_ref[positions:, :width] = values.astype(vs_ref.dtype)
    vs_ref[positions:, width:] = jnp.where(row < 2 * fresh, 1.0, 0.0).astype(vs_ref.dtype)

    lane = lax.broadcasted_iota(jnp.int32, (1, LANES), 1)
    mine = jnp.full((1, LANES), 2**30, jnp.int32)
    start = (place_ref[0] * Y + place_ref[1]) * fresh
    for j in range(2 * fresh):
        mine = jnp.where(lane == j, offsets_ref[start + j % fresh], mine)
    for y in range(Y):
        for z in range(Z):
            for n in range(fresh):
                seen = mine <= offsets_ref[(z_at(z) * Y + y) * fresh + n]
                at = (y * Z + z) * fresh + n
                vis_ref[at : at + 1, :] = jnp.where(seen, 1.0, 0.0)
    ks_ref[positions + LANES :, :] = vis_ref[...].astype(ks_ref.dtype)


def attend_kernel(whose, place_ref, q_ref, ks_ref, vs_ref, *refs):
    peers, _, per, width = q_ref.shape
    block = peers * per
    rows = block * len(whose)
    out_refs = refs[-len(whose) :]
    y = place_ref[1]
    owners = [(y, Y - 1 - y, lax.rem(y + 2, Y), y + 1 - 2 * lax.rem(y, 2))[which] for which in whose]
    positions = vs_ref.shape[0] - LANES
    tokens = block // 8
    groups = block // 8
    factor = log2_scale(width)
    query = jnp.concatenate([q_ref[:, lax.rem(lax.div(owner, YL) + YH - YH_FIRST, YH)].reshape(block, width) for owner in owners], axis=0)

    tops, parts = [], []
    for b in range(positions // KBLK):
        here = slice(b * KBLK, (b + 1) * KBLK)
        scores = lax.dot_general(query, ks_ref[here, :], NT, preferred_element_type=jnp.float32)
        top = jnp.max(scores, axis=1, keepdims=True)
        probs = jnp.exp2(scores * factor - top * factor).astype(jnp.bfloat16)
        tops.append(top)
        parts.append(jnp.dot(probs, vs_ref[here, :], preferred_element_type=jnp.float32))

    fresh = slice(positions, positions + LANES)
    scores = lax.dot_general(query, ks_ref[fresh, :], NT, preferred_element_type=jnp.float32)
    seen = [ks_ref[pl.ds(pl.multiple_of(fresh.stop + owner * tokens, tokens), tokens), :] for owner in owners]
    seen = jnp.concatenate([rows_seen.astype(jnp.float32) for rows_seen in seen], axis=0)
    seen = jnp.broadcast_to(seen[:, None, :], (rows // 8, 8, LANES)).reshape(rows, LANES) > 0
    scores = jnp.where(seen, scores, NEG)
    top = jnp.max(scores, axis=1, keepdims=True)
    probs = jnp.where(seen, jnp.exp2((scores - top) * factor), 0.0)
    rounded = probs.astype(jnp.bfloat16).astype(jnp.float32)
    lane = lax.broadcasted_iota(jnp.int32, (rows, LANES), 1)
    both = jnp.where(lane < 4, rounded, probs - rounded).astype(jnp.bfloat16)
    tops.append(top)
    parts.append(jnp.dot(both, vs_ref[fresh, :], preferred_element_type=jnp.float32))

    top = functools.reduce(jnp.maximum, tops)
    acc = functools.reduce(jnp.add, [part * jnp.exp2((t - top) * factor) for t, part in zip(tops, parts)])
    top = jnp.broadcast_to(top, (rows, LANES))

    lane = lax.broadcasted_iota(jnp.int32, (8, LANES), 1)
    for i, out_ref in enumerate(out_refs):
        start = i * block
        out_ref[:block, :] = acc[start : start + block, :width]
        stat = jnp.zeros((8, LANES), jnp.float32)
        for v in range(groups):
            at = slice(start + v * 8, start + v * 8 + 8)
            stat = jnp.where(lane == v, top[at, :], stat)
            stat = jnp.where(lane == groups + v, acc[at, width:], stat)
        out_ref[block:, :] = stat


def spread(stat, lane, width):
    return jnp.broadcast_to(stat[:, lane : lane + 1], (8, width))


def combine(refs, row, groups, width):
    rows = groups * 8
    g = row // 8
    stats = [ref[rows:, :] for ref in refs]
    tops = [spread(s, g, width) for s in stats]
    upper = functools.reduce(jnp.maximum, tops)
    out = jnp.zeros((8, width), jnp.float32)
    total = jnp.zeros((8, width), jnp.float32)
    for ref, s, t in zip(refs, stats, tops):
        weight = jnp.exp2((t - upper) * log2_scale(width))
        out = out + ref[row : row + 8, :] * weight
        total = total + spread(s, groups + g, width) * weight
    return out, upper, total


def pair_kernel(a_ref, b_ref, out_ref):
    rows, width = out_ref.shape
    rows = rows - STAT
    groups = rows // 8
    lane = lax.broadcasted_iota(jnp.int32, (8, LANES), 1)
    stat = jnp.zeros((8, LANES), jnp.float32)
    for g in range(groups):
        out, upper, total = combine((a_ref, b_ref), g * 8, groups, width)
        out_ref[g * 8 : g * 8 + 8, :] = out
        stat = jnp.where(lane == g, upper, stat)
        stat = jnp.where(lane == groups + g, total, stat)
    out_ref[rows:, :] = stat


def combine_kernel(a_ref, b_ref, c_ref, out_ref):
    peers, chunk_rows, width = out_ref.shape
    per = chunk_rows - STAT
    groups = peers * per // 8
    local = per // 8
    lane = lax.broadcasted_iota(jnp.int32, (8, LANES), 1)
    for p in range(peers):
        stat = jnp.zeros((8, LANES), jnp.float32)
        place = (p + Z_MERGE - Z_FIRST) % Z
        for v in range(local):
            out, upper, total = combine((a_ref, b_ref, c_ref), place * per + v * 8, groups, width)
            out_ref[p, v * 8 : v * 8 + 8, :] = out
            stat = jnp.where(lane == v, upper, stat)
            stat = jnp.where(lane == local + v, total, stat)
        out_ref[p, per:, :] = stat


def merge_kernel(in_ref, out_ref, row_ref):
    sources, chunk_rows, width = in_ref.shape
    per = chunk_rows - STAT
    groups = per // 8
    factor = log2_scale(width)
    stat = in_ref[:, per:, :]
    for v in range(groups):
        tops = jnp.broadcast_to(stat[:, :, v : v + 1], (sources, 8, width))
        totals = jnp.broadcast_to(stat[:, :, groups + v : groups + v + 1], (sources, 8, width))
        upper = jnp.max(tops, axis=0)
        weight = jnp.exp2((tops - upper[None]) * factor)
        out = jnp.sum(in_ref[:, v * 8 : v * 8 + 8, :] * weight, axis=0)
        out = out / jnp.sum(totals * weight, axis=0)
        for g in range(8):
            row_ref[v : v + 1, g * width : (g + 1) * width] = out[g : g + 1, :]
    row = row_ref[...]
    for c in range(out_ref.shape[1] // row.shape[1]):
        out_ref[:, c * row.shape[1] : (c + 1) * row.shape[1]] = row


def shards(queries, new_keys, new_values, cache_keys, cache_values, cache_lengths, offsets):
    heads = X * CORE
    rows, _, group, width = queries.shape
    per = rows * group
    positions = cache_keys.shape[1]
    vmem = pl.BlockSpec(memory_space=pltpu.VMEM)
    smem = pl.BlockSpec(memory_space=pltpu.SMEM)
    anywhere = pl.BlockSpec(memory_space=pl.ANY)
    params = pltpu.CompilerParams(vmem_limit_bytes=VMEM_LIMIT)
    ring = ("yh", "yl")
    place = jnp.stack([lax.axis_index("z"), lax.axis_index(ring)]).astype(jnp.int32)

    def swap(block, partner):
        return lax.ppermute(block, ring, [(y, partner(y)) for y in range(Y)])

    def across(y):
        return Y - 1 - y

    def beside(y):
        return y ^ 1

    with jax.named_scope("gather_queries"):
        mine = queries.reshape(per, width)
        order = [[z_at(i) * YH + (yh + YH_FIRST) % YH for i in range(Z) for yh in range(YH)]]
        copies = jnp.broadcast_to(mine[None], (Z * YH, per, width))
        same = lax.all_to_all(copies, ("z", "yh"), 0, 0, axis_index_groups=order)
        same = same.reshape(Z, YH, per, width)

    with jax.named_scope("prepare"):
        new = jnp.concatenate([new_keys[:, 0], new_values[:, 0]], axis=0)
        keys, values = pl.pallas_call(
            prepare_kernel,
            out_shape=(
                jax.ShapeDtypeStruct((positions + LANES + Z * Y * rows, width), cache_keys.dtype),
                jax.ShapeDtypeStruct((positions + LANES, 2 * width), cache_values.dtype),
            ),
            in_specs=[smem] * 3 + [vmem] * 3,
            out_specs=[vmem] * 2,
            scratch_shapes=[pltpu.VMEM((Z * Y * rows, LANES), jnp.float32)],
            compiler_params=params,
        )(place, cache_lengths, offsets, cache_keys[0], cache_values[0], new)

    with jax.named_scope("swap_parity"):
        same, keys, values = lax.optimization_barrier((same, keys, values))
        other = lax.ppermute(same, "yl", [(0, 1), (1, 0)])

    def attend(backs, rows_in, *after):
        return pl.pallas_call(
            functools.partial(attend_kernel, backs),
            out_shape=[jax.ShapeDtypeStruct((Z * per + STAT, width), jnp.float32)] * len(backs),
            in_specs=[smem] + [vmem] * 3 + [anywhere] * len(after),
            out_specs=[vmem] * len(backs),
            compiler_params=params,
            cost_estimate=pl.CostEstimate(
                flops=4 * len(backs) * Z * per * positions * 4 * width,
                transcendentals=len(backs) * Z * per * positions,
                bytes_accessed=8 * positions * width,
            ),
        )(place, rows_in, keys, values, *after)

    with jax.named_scope("attend_two_on"):
        (two_on,) = attend((OPPOSITE,), same)
        passing = swap(two_on, across)
    with jax.named_scope("attend_neighbours"):
        for_across, for_beside = attend((ACROSS, BESIDE), other, two_on)
        from_across = swap(for_across, across)
    with jax.named_scope("pass_on"):
        for_beside = pl.pallas_call(
            pair_kernel,
            out_shape=jax.ShapeDtypeStruct(for_beside.shape, jnp.float32),
            in_specs=[vmem] * 2,
            out_specs=vmem,
            compiler_params=params,
        )(for_beside, passing)
        from_beside = swap(for_beside, beside)
    with jax.named_scope("attend_own"):
        (own,) = attend((OWN,), same, for_beside)

    with jax.named_scope("combine"):
        column = pl.pallas_call(
            combine_kernel,
            out_shape=jax.ShapeDtypeStruct((Z, per + STAT, width), jnp.float32),
            in_specs=[vmem] * 3,
            out_specs=vmem,
            compiler_params=params,
        )(own, from_across, from_beside)

    with jax.named_scope("exchange_z"):
        order = [[(i + Z_MERGE) % Z for i in range(Z)]]
        arrived = lax.all_to_all(column, "z", 0, 0, axis_index_groups=order)

    with jax.named_scope("merge"):
        merged = pl.pallas_call(
            merge_kernel,
            out_shape=jax.ShapeDtypeStruct((rows, heads * group * width), jnp.float32),
            in_specs=[vmem],
            out_specs=vmem,
            scratch_shapes=[pltpu.VMEM((rows, group * width), jnp.float32)],
            compiler_params=params,
        )(arrived)

    with jax.named_scope("gather_heads"):
        order = [[(i + HEAD_FIRST) % heads for i in range(heads)]]
        whole = lax.all_to_all(merged, ("x", "core"), 1, 1, tiled=True, axis_index_groups=order)
        return jnp.roll(whole, HEAD_FIRST * group * width, axis=1)


def solution(mesh):
    grid = Mesh(mesh.devices.reshape(Z, YH, YL, X, CORE), ("z", "yh", "yl", "x", "core"))
    ctx, kvh = ("z", "yh", "yl"), ("x", "core")
    return jax.shard_map(
        shards,
        mesh=grid,
        in_specs=(
            P(ctx, kvh, None, None),
            P(ctx, kvh, None),
            P(ctx, kvh, None),
            P(kvh, ctx, None),
            P(kvh, ctx, None),
            P(ctx),
            P(),
        ),
        out_specs=P(ctx, None),
        check_vma=False,
    )
```

```python
import functools
import math

import jax
import jax.numpy as jnp
from jax import lax
from jax.experimental import pallas as pl
from jax.experimental.pallas import tpu as pltpu
from jax.sharding import Mesh
from jax.sharding import PartitionSpec as P

KBLK = 512
NEG = -1e30
LANES = 128
STAT = 8
NT = (((1,), (1,)), ((), ()))
Z, YH, YL, X, CORE = 8, 2, 2, 4, 2
Y = YH * YL
Z_FIRST, YH_FIRST = 5, 1
Z_MERGE = 5
HEAD_FIRST = 5
OWN, ACROSS, OPPOSITE, BESIDE = range(4)
VMEM_LIMIT = 24 * 2**20


def z_at(i):
    return (i + Z_FIRST) % Z


def log2_scale(width):
    return width**-0.5 * math.log2(math.e)


def prepare_kernel(place_ref, length_ref, offsets_ref, k_ref, v_ref, new_ref, ks_ref, vs_ref, vis_ref):
    positions, width = k_ref.shape
    fresh = new_ref.shape[0] // 2
    length = length_ref[0]
    ones = jnp.ones((KBLK, width), vs_ref.dtype)
    for b in range(positions // KBLK):
        here = slice(b * KBLK, (b + 1) * KBLK)

        @pl.when((b + 1) * KBLK <= length)
        def _():
            ks_ref[here, :] = k_ref[here, :]
            vs_ref[here, :width] = v_ref[here, :]
            vs_ref[here, width:] = ones

        @pl.when((b + 1) * KBLK > length)
        def _():
            inside = b * KBLK + lax.broadcasted_iota(jnp.int32, (KBLK, width), 0) < length
            first = k_ref[0:16, :].astype(jnp.float32)[0:1, :]
            keys = jnp.where(inside, k_ref[here, :].astype(jnp.float32), first)
            values = jnp.where(inside, v_ref[here, :].astype(jnp.float32), 0.0)
            ks_ref[here, :] = keys.astype(ks_ref.dtype)
            vs_ref[here, :width] = values.astype(vs_ref.dtype)
            vs_ref[here, width:] = jnp.where(inside, 1.0, 0.0).astype(vs_ref.dtype)

    row = lax.broadcasted_iota(jnp.int32, (LANES, width), 0)
    keys = jnp.zeros((LANES, width), jnp.float32)
    values = jnp.zeros((LANES, width), jnp.float32)
    new = new_ref[...].astype(jnp.float32)
    for j in range(2 * fresh):
        n = j % fresh
        keys = jnp.where(row == j, new[n : n + 1, :], keys)
        values = jnp.where(row == j, new[fresh + n : fresh + n + 1, :], values)
    ks_ref[positions : positions + LANES, :] = keys.astype(ks_ref.dtype)
    vs_ref[positions:, :width] = values.astype(vs_ref.dtype)
    vs_ref[positions:, width:] = jnp.where(row < 2 * fresh, 1.0, 0.0).astype(vs_ref.dtype)

    lane = lax.broadcasted_iota(jnp.int32, (1, LANES), 1)
    mine = jnp.full((1, LANES), 2**30, jnp.int32)
    start = (place_ref[0] * Y + place_ref[1]) * fresh
    for j in range(2 * fresh):
        mine = jnp.where(lane == j, offsets_ref[start + j % fresh], mine)
    for y in range(Y):
        for z in range(Z):
            for n in range(fresh):
                seen = mine <= offsets_ref[(z_at(z) * Y + y) * fresh + n]
                at = (y * Z + z) * fresh + n
                vis_ref[at : at + 1, :] = jnp.where(seen, 1.0, 0.0)
    ks_ref[positions + LANES :, :] = vis_ref[...].astype(ks_ref.dtype)


def attend_kernel(whose, place_ref, q_ref, ks_ref, vs_ref, *refs):
    peers, _, per, width = q_ref.shape
    block = peers * per
    rows = block * len(whose)
    out_refs = refs[-len(whose) :]
    y = place_ref[1]
    owners = [(y, Y - 1 - y, lax.rem(y + 2, Y), y + 1 - 2 * lax.rem(y, 2))[which] for which in whose]
    positions = vs_ref.shape[0] - LANES
    tokens = block // 8
    groups = block // 8
    factor = log2_scale(width)
    query = jnp.concatenate([q_ref[:, lax.rem(lax.div(owner, YL) + YH - YH_FIRST, YH)].reshape(block, width) for owner in owners], axis=0)

    tops, parts = [], []
    for b in range(positions // KBLK):
        here = slice(b * KBLK, (b + 1) * KBLK)
        scores = lax.dot_general(query, ks_ref[here, :], NT, preferred_element_type=jnp.float32)
        top = jnp.max(scores, axis=1, keepdims=True)
        probs = jnp.exp2(scores * factor - top * factor).astype(jnp.bfloat16)
        tops.append(top)
        parts.append(jnp.dot(probs, vs_ref[here, :], preferred_element_type=jnp.float32))

    fresh = slice(positions, positions + LANES)
    scores = lax.dot_general(query, ks_ref[fresh, :], NT, preferred_element_type=jnp.float32)
    seen = [ks_ref[pl.ds(pl.multiple_of(fresh.stop + owner * tokens, tokens), tokens), :] for owner in owners]
    seen = jnp.concatenate([rows_seen.astype(jnp.float32) for rows_seen in seen], axis=0)
    seen = jnp.broadcast_to(seen[:, None, :], (rows // 8, 8, LANES)).reshape(rows, LANES) > 0
    scores = jnp.where(seen, scores, NEG)
    top = jnp.max(scores, axis=1, keepdims=True)
    probs = jnp.where(seen, jnp.exp2((scores - top) * factor), 0.0)
    rounded = probs.astype(jnp.bfloat16).astype(jnp.float32)
    lane = lax.broadcasted_iota(jnp.int32, (rows, LANES), 1)
    both = jnp.where(lane < 4, rounded, probs - rounded).astype(jnp.bfloat16)
    tops.append(top)
    parts.append(jnp.dot(both, vs_ref[fresh, :], preferred_element_type=jnp.float32))

    top = functools.reduce(jnp.maximum, tops)
    acc = functools.reduce(jnp.add, [part * jnp.exp2((t - top) * factor) for t, part in zip(tops, parts)])
    top = jnp.broadcast_to(top, (rows, LANES))

    lane = lax.broadcasted_iota(jnp.int32, (8, LANES), 1)
    for i, out_ref in enumerate(out_refs):
        start = i * block
        out_ref[:block, :] = acc[start : start + block, :width]
        chains = [jnp.zeros((8, LANES), jnp.float32) for _ in range(8)]
        for v in range(groups):
            at = slice(start + v * 8, start + v * 8 + 8)
            k = v % 4
            chains[k] = jnp.where(lane == v, top[at, :], chains[k])
            chains[4 + k] = jnp.where(lane == groups + v, acc[at, width:], chains[4 + k])
        out_ref[block:, :] = functools.reduce(jnp.add, chains)


def spread(stat, lane, width):
    return jnp.broadcast_to(stat[:, lane : lane + 1], (8, width))


def combine(refs, row, groups, width):
    rows = groups * 8
    g = row // 8
    stats = [ref[rows:, :] for ref in refs]
    tops = [spread(s, g, width) for s in stats]
    upper = functools.reduce(jnp.maximum, tops)
    out = jnp.zeros((8, width), jnp.float32)
    total = jnp.zeros((8, width), jnp.float32)
    for ref, s, t in zip(refs, stats, tops):
        weight = jnp.exp2((t - upper) * log2_scale(width))
        out = out + ref[row : row + 8, :] * weight
        total = total + spread(s, groups + g, width) * weight
    return out, upper, total


def pair_kernel(a_ref, b_ref, out_ref):
    rows, width = out_ref.shape
    rows = rows - STAT
    groups = rows // 8
    lane = lax.broadcasted_iota(jnp.int32, (8, LANES), 1)
    stat = jnp.zeros((8, LANES), jnp.float32)
    for g in range(groups):
        out, upper, total = combine((a_ref, b_ref), g * 8, groups, width)
        out_ref[g * 8 : g * 8 + 8, :] = out
        stat = jnp.where(lane == g, upper, stat)
        stat = jnp.where(lane == groups + g, total, stat)
    out_ref[rows:, :] = stat


def combine_kernel(a_ref, b_ref, c_ref, out_ref):
    peers, chunk_rows, width = out_ref.shape
    per = chunk_rows - STAT
    groups = peers * per // 8
    local = per // 8
    lane = lax.broadcasted_iota(jnp.int32, (8, LANES), 1)
    for p in range(peers):
        stat = jnp.zeros((8, LANES), jnp.float32)
        place = (p + Z_MERGE - Z_FIRST) % Z
        for v in range(local):
            out, upper, total = combine((a_ref, b_ref, c_ref), place * per + v * 8, groups, width)
            out_ref[p, v * 8 : v * 8 + 8, :] = out
            stat = jnp.where(lane == v, upper, stat)
            stat = jnp.where(lane == local + v, total, stat)
        out_ref[p, per:, :] = stat


def merge_kernel(in_ref, out_ref, row_ref):
    sources, chunk_rows, width = in_ref.shape
    per = chunk_rows - STAT
    groups = per // 8
    factor = log2_scale(width)
    stat = in_ref[:, per:, :]
    for v in range(groups):
        tops = jnp.broadcast_to(stat[:, :, v : v + 1], (sources, 8, width))
        totals = jnp.broadcast_to(stat[:, :, groups + v : groups + v + 1], (sources, 8, width))
        upper = jnp.max(tops, axis=0)
        weight = jnp.exp2((tops - upper[None]) * factor)
        out = jnp.sum(in_ref[:, v * 8 : v * 8 + 8, :] * weight, axis=0)
        out = out / jnp.sum(totals * weight, axis=0)
        for g in range(8):
            row_ref[v : v + 1, g * width : (g + 1) * width] = out[g : g + 1, :]
    row = row_ref[...]
    for c in range(out_ref.shape[1] // row.shape[1]):
        out_ref[:, c * row.shape[1] : (c + 1) * row.shape[1]] = row


def shards(queries, new_keys, new_values, cache_keys, cache_values, cache_lengths, offsets):
    heads = X * CORE
    rows, _, group, width = queries.shape
    per = rows * group
    positions = cache_keys.shape[1]
    vmem = pl.BlockSpec(memory_space=pltpu.VMEM)
    smem = pl.BlockSpec(memory_space=pltpu.SMEM)
    anywhere = pl.BlockSpec(memory_space=pl.ANY)
    params = pltpu.CompilerParams(vmem_limit_bytes=VMEM_LIMIT)
    ring = ("yh", "yl")
    place = jnp.stack([lax.axis_index("z"), lax.axis_index(ring)]).astype(jnp.int32)

    def swap(block, partner):
        return lax.ppermute(block, ring, [(y, partner(y)) for y in range(Y)])

    def across(y):
        return Y - 1 - y

    def beside(y):
        return y ^ 1

    with jax.named_scope("gather_queries"):
        mine = queries.reshape(per, width)
        order = [[z_at(i) * YH + (yh + YH_FIRST) % YH for i in range(Z) for yh in range(YH)]]
        copies = jnp.broadcast_to(mine[None], (Z * YH, per, width))
        same = lax.all_to_all(copies, ("z", "yh"), 0, 0, axis_index_groups=order)
        same = same.reshape(Z, YH, per, width)

    with jax.named_scope("prepare"):
        new = jnp.concatenate([new_keys[:, 0], new_values[:, 0]], axis=0)
        keys, values = pl.pallas_call(
            prepare_kernel,
            out_shape=(
                jax.ShapeDtypeStruct((positions + LANES + Z * Y * rows, width), cache_keys.dtype),
                jax.ShapeDtypeStruct((positions + LANES, 2 * width), cache_values.dtype),
            ),
            in_specs=[smem] * 3 + [vmem] * 3,
            out_specs=[vmem] * 2,
            scratch_shapes=[pltpu.VMEM((Z * Y * rows, LANES), jnp.float32)],
            compiler_params=params,
        )(place, cache_lengths, offsets, cache_keys[0], cache_values[0], new)

    with jax.named_scope("swap_parity"):
        same, keys, values = lax.optimization_barrier((same, keys, values))
        other = lax.ppermute(same, "yl", [(0, 1), (1, 0)])

    def attend(backs, rows_in, *after):
        return pl.pallas_call(
            functools.partial(attend_kernel, backs),
            out_shape=[jax.ShapeDtypeStruct((Z * per + STAT, width), jnp.float32)] * len(backs),
            in_specs=[smem] + [vmem] * 3 + [anywhere] * len(after),
            out_specs=[vmem] * len(backs),
            compiler_params=params,
            cost_estimate=pl.CostEstimate(
                flops=4 * len(backs) * Z * per * positions * 4 * width,
                transcendentals=len(backs) * Z * per * positions,
                bytes_accessed=8 * positions * width,
            ),
        )(place, rows_in, keys, values, *after)

    with jax.named_scope("attend_two_on"):
        (two_on,) = attend((OPPOSITE,), same)
        passing = swap(two_on, across)
    with jax.named_scope("attend_neighbours"):
        for_across, for_beside = attend((ACROSS, BESIDE), other, two_on)
        from_across = swap(for_across, across)
    with jax.named_scope("pass_on"):
        for_beside = pl.pallas_call(
            pair_kernel,
            out_shape=jax.ShapeDtypeStruct(for_beside.shape, jnp.float32),
            in_specs=[vmem] * 2,
            out_specs=vmem,
            compiler_params=params,
        )(for_beside, passing)
        from_beside = swap(for_beside, beside)
    with jax.named_scope("attend_own"):
        (own,) = attend((OWN,), same, for_beside)

    with jax.named_scope("combine"):
        column = pl.pallas_call(
            combine_kernel,
            out_shape=jax.ShapeDtypeStruct((Z, per + STAT, width), jnp.float32),
            in_specs=[vmem] * 3,
            out_specs=vmem,
            compiler_params=params,
        )(own, from_across, from_beside)

    with jax.named_scope("exchange_z"):
        order = [[(i + Z_MERGE) % Z for i in range(Z)]]
        arrived = lax.all_to_all(column, "z", 0, 0, axis_index_groups=order)

    with jax.named_scope("merge"):
        merged = pl.pallas_call(
            merge_kernel,
            out_shape=jax.ShapeDtypeStruct((rows, heads * group * width), jnp.float32),
            in_specs=[vmem],
            out_specs=vmem,
            scratch_shapes=[pltpu.VMEM((rows, group * width), jnp.float32)],
            compiler_params=params,
        )(arrived)

    with jax.named_scope("gather_heads"):
        order = [[(i + HEAD_FIRST) % heads for i in range(heads)]]
        whole = lax.all_to_all(merged, ("x", "core"), 1, 1, tiled=True, axis_index_groups=order)
        return jnp.roll(whole, HEAD_FIRST * group * width, axis=1)


def solution(mesh):
    grid = Mesh(mesh.devices.reshape(Z, YH, YL, X, CORE), ("z", "yh", "yl", "x", "core"))
    ctx, kvh = ("z", "yh", "yl"), ("x", "core")
    return jax.shard_map(
        shards,
        mesh=grid,
        in_specs=(
            P(ctx, kvh, None, None),
            P(ctx, kvh, None),
            P(ctx, kvh, None),
            P(kvh, ctx, None),
            P(kvh, ctx, None),
            P(ctx),
            P(),
        ),
        out_specs=P(ctx, None),
        check_vma=False,
    )
```
